256 devices in a mesh: orb: 64 (over z, x, core), pair: 4 (over y).
Axes of the slice: x: 4, y: 4, z: 8, core: 2. Of those that a mesh axis runs over, the one named last changes fastest.
Arguments:
- integrals: bfloat16 [2048, 1024, 256], P(('orb', 'pair')), may hold values from -2 to 2
- fock_blocks: bfloat16 [1024, 256, 256], P(('orb', 'pair')), as said below
- occ_energy: float32 [1024], P('orb'), may hold values from -2 to -0.3
- dom_len: int32 [1024], P('orb'), may hold values from 85 to 256, as said below
- amplitudes: bfloat16 [4096, 256, 256], P(('orb', 'pair')), may hold values from -1.796875 to 1.796875
- pair_list: int32 [4096, 2], P('orb'), may hold values from 0 to 15, as said below
Outputs:
- residual: bfloat16 [4096, 256, 256], P(('orb', 'pair'))
- new_amplitudes: bfloat16 [4096, 256, 256], P(('orb', 'pair'))
The draws below stay inside these ranges and needn't reach their ends.
Inputs may be any that keep to these rules, and one draw needn't show every extreme that they name: `pair_list`: rows g * 64 to g * 64 + 63 hold the pairs of group g; each row names two orbital numbers with the first not above the second, and no row repeats within a group. `dom_len`: the largest length is 256 in every draw. `fock_blocks`: diagonal entries lie between 1 and 3.
All inputs are finite; a program needn't handle non-finite values.
Results may differ from the reference program's by a relative error of at most 0.001.
Values may be sent and summed in bfloat16 or wider, within the bound.
No kernel may reach another device: no remote copies, remote signals or barrier semaphores. Data moves between devices by JAX's collectives and lax.ppermute only.
A program may use at most 192 MiB of HBM per device.

```python
import jax
import jax.numpy as jnp
import numpy as np
from jax import lax

DOM = 256
PAIR_DEV = 16
GRP_ORB = 16
OCC = 1024
NAUX = 2048
PAIRS_GRP = 64
PAIRS = 4096


def draw_fock_blocks(key, part):
    key = jax.random.fold_in(key, 11)
    key_diag, key_off = jax.random.split(key)
    diag = jax.random.uniform(key_diag, (OCC, DOM), jnp.float32, 1.0, 3.0)
    off = jnp.clip(jax.random.normal(key_off, (OCC, DOM, DOM), jnp.float32), -4.0, 4.0) * (0.6 / DOM ** 0.5)
    eye = jnp.eye(DOM, dtype=jnp.float32)
    blocks = off * (1.0 - eye) + eye * diag[:, None, :]
    return blocks.astype(jnp.bfloat16)


def draw_dom_len(key, part):
    key = jax.random.fold_in(key, 23)
    key_len, key_where = jax.random.split(key)
    lengths = jax.random.randint(key_len, (OCC,), DOM // 3, DOM + 1, jnp.int32)
    where = jax.random.randint(key_where, (), 0, OCC, jnp.int32)
    lengths = jnp.where(jnp.arange(OCC, dtype=jnp.int32) == where, DOM, lengths)
    return lengths.astype(jnp.int32)


def draw_pair_list(key, part):
    key = jax.random.fold_in(key, 37)
    upper = np.stack(np.triu_indices(GRP_ORB), axis=1).astype(np.int32)
    count = upper.shape[0]
    keys = jax.random.split(key, PAIRS // PAIRS_GRP)
    picks = jax.vmap(lambda k: jax.random.permutation(k, count)[:PAIRS_GRP])(keys)
    table = jnp.asarray(upper)
    return table[picks.reshape(-1)].reshape(PAIRS, 2).astype(jnp.int32)


def block_scale(stream_key, dims, shards, smallest, top_value):
    factor_of, own = 1.0, jax.random.fold_in(stream_key, 6)
    for dim, blocks in shards:
        draws = jnp.exp(jax.random.uniform(jax.random.fold_in(own, dim), (blocks,), jnp.float32, smallest / len(shards), top_value / len(shards)))
        factor_of = factor_of * jnp.repeat(draws, dims[dim] // blocks).reshape([-1 if axis == dim else 1 for axis in range(len(dims))])
    return factor_of


def noise(key, extent, spread, limit, shards=(), held_as=jnp.bfloat16):
    array = spread * jax.random.normal(key, extent, jnp.float32)
    if shards:
        array = array * block_scale(key, extent, shards, -0.22, 0.18)
    return jnp.clip(array, -limit, limit).astype(held_as)


def setup_inputs(seed: int = 0) -> dict:
    seeds = jax.random.split(jax.random.key(seed), 7)
    return {
        "integrals": noise(seeds[0], (NAUX, OCC, DOM), (NAUX ** -0.25), 2.0, ((0, 256),)),
        "fock_blocks": draw_fock_blocks(jax.random.fold_in(seeds[6], 71), 0),
        "occ_energy": jnp.clip(-2.0 + 1.7 * jax.random.uniform(seeds[2], (OCC,), jnp.float32) ** block_scale(seeds[2], (OCC,), ((0, 64),), -0.2, 0.2), -2.0, -0.3),
        "dom_len": draw_dom_len(jax.random.fold_in(seeds[6], 71), 0),
        "amplitudes": noise(seeds[4], (PAIRS, DOM, DOM), 0.3, 1.796875, ((0, 256),)),
        "pair_list": draw_pair_list(jax.random.fold_in(seeds[6], 71), 0),
    }


def reference(integrals, fock_blocks, occ_energy, dom_len, amplitudes, pair_list):
    group = jnp.arange(PAIRS, dtype=jnp.int32) // PAIRS_GRP
    first_all = (group * GRP_ORB + pair_list[:, 0]).astype(jnp.int32)
    second_all = (group * GRP_ORB + pair_list[:, 1]).astype(jnp.int32)
    blocks = PAIRS // PAIR_DEV
    positions = jnp.arange(DOM, dtype=jnp.int32)

    def one_block(index):
        begin = (index * PAIR_DEV).astype(jnp.int32)
        first = lax.dynamic_slice_in_dim(first_all, begin, PAIR_DEV, 0)
        second = lax.dynamic_slice_in_dim(second_all, begin, PAIR_DEV, 0)
        old = lax.dynamic_slice_in_dim(amplitudes, begin, PAIR_DEV, 0).astype(jnp.float32)
        left = jnp.take(integrals, first, axis=1).astype(jnp.float32)
        right = jnp.take(integrals, second, axis=1).astype(jnp.float32)
        exchange = jnp.einsum("qpa,qpb->pab", left, right)
        fock_first = jnp.take(fock_blocks, first, axis=0).astype(jnp.float32)
        fock_second = jnp.take(fock_blocks, second, axis=0).astype(jnp.float32)
        left_term = jnp.einsum("pac,pcb->pab", fock_first, old)
        right_term = jnp.einsum("pac,pbc->pab", old, fock_second)
        energies = jnp.take(occ_energy, first) + jnp.take(occ_energy, second)
        inside_first = positions[None, :] < jnp.take(dom_len, first)[:, None]
        inside_second = positions[None, :] < jnp.take(dom_len, second)[:, None]
        mask = (inside_first[:, :, None] & inside_second[:, None, :]).astype(jnp.float32)
        resid = mask * (exchange + left_term + right_term - energies[:, None, None] * old)
        diag_first = jnp.diagonal(fock_first, axis1=1, axis2=2)
        diag_second = jnp.diagonal(fock_second, axis1=1, axis2=2)
        denominator = diag_first[:, :, None] + diag_second[:, None, :] - energies[:, None, None]
        updated = mask * (old - resid / denominator)
        return resid.astype(jnp.bfloat16), updated.astype(jnp.bfloat16)

    resid, updated = lax.map(one_block, jnp.arange(blocks, dtype=jnp.int32))
    return resid.reshape(PAIRS, DOM, DOM), updated.reshape(PAIRS, DOM, DOM)
```

```python
import functools

import jax
import jax.numpy as jnp
from jax import lax
from jax.experimental import pallas as pl
from jax.experimental.pallas import tpu as pltpu
from jax.sharding import PartitionSpec as P

BOTH = ("orb", "pair")
SPLITS = ((0, 12), (12, 16))
VMEM = 24 * 2**20


def gather_mate(orb, y):
    return y ^ 1 if orb % 2 == 0 else 3 - y


def sum_mate(orb, y):
    return 3 - y if orb % 2 == 0 else y ^ 1


def exchange_with(x, mate, orbs, ys):
    pairs = [(o * ys + y, o * ys + mate(o, y)) for o in range(orbs) for y in range(ys)]
    return lax.ppermute(x, BOTH, pairs)


def load_blocks(parts, held, sems):
    copies = []
    for half in range(2):
        for c, (lo, hi) in enumerate(SPLITS):
            k = half * len(SPLITS) + c
            copies.append(
                pltpu.make_async_copy(parts[k], held.at[half, :, lo:hi], sems.at[k])
            )
    return copies


def half_sum(held, i, j):
    total = None
    for half in range(2):
        left = held[half, :, i].reshape(-1, held.shape[-1])
        right = held[half, :, j].reshape(-1, held.shape[-1])
        term = lax.dot_general(
            left, right, (((0,), (0,)), ((), ())), preferred_element_type=jnp.float32
        )
        total = term if total is None else total + term
    return total


def partial_kernel(first, pairs_ref, begin_ref, *refs):
    parts, out_refs, held, sems = refs[:4], refs[4:-2], refs[-2], refs[-1]
    p = pl.program_id(0)

    @pl.when(p == 0)
    def _():
        copies = load_blocks(parts, held, sems)
        for c in copies:
            c.start()
        for c in copies:
            c.wait()

    row = begin_ref[0] + first + p
    out_refs[0][0] = half_sum(held, pairs_ref[2 * row], pairs_ref[2 * row + 1])


def partial_sums(parts, pairs, begin, first, count):
    _, _, aux, dom = parts[0].shape
    orbs = SPLITS[-1][1]
    src = parts[0].shape[0]
    return pl.pallas_call(
        functools.partial(partial_kernel, first),
        grid_spec=pltpu.PrefetchScalarGridSpec(
            num_scalar_prefetch=2,
            grid=(count,),
            in_specs=[pl.BlockSpec(memory_space=pl.ANY)] * 4,
            out_specs=[pl.BlockSpec((1, dom, dom), lambda p, *_: (p, 0, 0))],
            scratch_shapes=[
                pltpu.VMEM((2, src, orbs, aux, dom), jnp.bfloat16),
                pltpu.SemaphoreType.DMA((4,)),
            ],
        ),
        out_shape=[jax.ShapeDtypeStruct((count, dom, dom), jnp.float32)],
        compiler_params=pltpu.CompilerParams(vmem_limit_bytes=VMEM),
        cost_estimate=pl.CostEstimate(
            flops=2 * count * 2 * src * aux * dom * dom * 4,
            bytes_accessed=4 * src * orbs * aux * dom + count * dom * dom * 4,
            transcendentals=0,
        ),
    )(pairs, begin, *parts)[0]


def own_kernel(pairs_ref, begin_ref, *refs):
    parts, base_ref, out_ref, held, sems = refs[:4], refs[4], refs[5], refs[6], refs[7]
    p = pl.program_id(0)

    @pl.when(p == 0)
    def _():
        copies = load_blocks(parts, held, sems)
        for c in copies:
            c.start()
        for c in copies:
            c.wait()

    row = begin_ref[0] + p
    out_ref[0] = base_ref[0] + half_sum(held, pairs_ref[2 * row], pairs_ref[2 * row + 1])


def own_sums(parts, base, pairs, begin):
    src, _, aux, dom = parts[0].shape
    orbs = SPLITS[-1][1]
    count = base.shape[0]
    one = pl.BlockSpec((1, dom, dom), lambda p, *_: (p, 0, 0))
    return pl.pallas_call(
        own_kernel,
        grid_spec=pltpu.PrefetchScalarGridSpec(
            num_scalar_prefetch=2,
            grid=(count,),
            in_specs=[pl.BlockSpec(memory_space=pl.ANY)] * 4 + [one],
            out_specs=[one],
            scratch_shapes=[
                pltpu.VMEM((2, src, orbs, aux, dom), jnp.bfloat16),
                pltpu.SemaphoreType.DMA((4,)),
            ],
        ),
        out_shape=[jax.ShapeDtypeStruct((count, dom, dom), jnp.float32)],
        input_output_aliases={6: 0},
        compiler_params=pltpu.CompilerParams(vmem_limit_bytes=VMEM),
        cost_estimate=pl.CostEstimate(
            flops=2 * count * 2 * src * aux * dom * dom * 4,
            bytes_accessed=4 * src * orbs * aux * dom + count * dom * dom * 8,
            transcendentals=0,
        ),
    )(pairs, begin, *parts, base)[0]


def fock_kernel(pairs_ref, begin_ref, slot_ref, occ_ref, len_ref, *refs):
    focks, amp_ref, base_ref, inv_ref, fock, sems = refs[:4], refs[4], *refs[5:]
    p = pl.program_id(0)
    dom = fock.shape[-1]

    @pl.when(p == 0)
    def _():
        each = focks[0].shape[0]
        copies = [
            pltpu.make_async_copy(
                focks[s], fock.at[s * each : (s + 1) * each], sems.at[s]
            )
            for s in range(4)
        ]
        for c in copies:
            c.start()
        for c in copies:
            c.wait()

    row = begin_ref[0] + p
    i = pairs_ref[2 * row]
    j = pairs_ref[2 * row + 1]
    energies = occ_ref[i] + occ_ref[j]
    old = amp_ref[0]
    fock_i = fock[slot_ref[i]]
    fock_j = fock[slot_ref[j]]
    total = jnp.dot(fock_i, old, preferred_element_type=jnp.float32)
    total += lax.dot_general(
        old, fock_j, (((1,), (1,)), ((), ())), preferred_element_type=jnp.float32
    )
    base_ref[0] = total - energies * old.astype(jnp.float32)
    rows = lax.broadcasted_iota(jnp.int32, (dom, dom), 0)
    columns = lax.broadcasted_iota(jnp.int32, (dom, dom), 1)
    eye = rows == columns
    diag_i = jnp.sum(
        jnp.where(eye, fock_i.astype(jnp.float32), 0.0), axis=1, keepdims=True
    )
    diag_j = jnp.sum(
        jnp.where(eye, fock_j.astype(jnp.float32), 0.0), axis=0, keepdims=True
    )
    inside = (rows < len_ref[i]) & (columns < len_ref[j])
    inv_ref[0] = jnp.where(inside, 1.0 / (diag_i + diag_j - energies), 0.0)


def fock_terms(focks, amplitudes, pairs, begin, slot, occ, lengths):
    count, dom, _ = amplitudes.shape
    one = pl.BlockSpec((1, dom, dom), lambda p, *_: (p, 0, 0))
    shape = jax.ShapeDtypeStruct((count, dom, dom), jnp.float32)
    return pl.pallas_call(
        fock_kernel,
        grid_spec=pltpu.PrefetchScalarGridSpec(
            num_scalar_prefetch=5,
            grid=(count,),
            in_specs=[pl.BlockSpec(memory_space=pl.ANY)] * 4 + [one],
            out_specs=[one, one],
            scratch_shapes=[
                pltpu.VMEM((4 * focks[0].shape[0], dom, dom), jnp.bfloat16),
                pltpu.SemaphoreType.DMA((4,)),
            ],
        ),
        out_shape=[shape, shape],
        compiler_params=pltpu.CompilerParams(vmem_limit_bytes=VMEM),
        cost_estimate=pl.CostEstimate(
            flops=2 * count * 2 * dom * dom * dom,
            bytes_accessed=count * dom * dom * 12,
            transcendentals=0,
        ),
    )(pairs, begin, slot, occ, lengths, *focks, amplitudes)


def finish_kernel(own_ref, other_ref, amp_ref, inv_ref, *refs):
    resid_ref, new_ref = refs[-2:]
    inv = inv_ref[0]
    inside = inv != 0.0
    resid = jnp.where(inside, own_ref[0] + other_ref[0], 0.0)
    old = amp_ref[0].astype(jnp.float32)
    resid_ref[0] = resid.astype(resid_ref.dtype)
    new_ref[0] = jnp.where(inside, old - resid * inv, 0.0).astype(new_ref.dtype)


def finish(own, other, amplitudes, inv, first, held):
    total, dom, _ = amplitudes.shape
    count = other.shape[0]
    shifted = pl.BlockSpec((1, dom, dom), lambda p: (p + first, 0, 0))
    shape = jax.ShapeDtypeStruct((total, dom, dom), jnp.bfloat16)
    extra = [] if held is None else list(held)
    return pl.pallas_call(
        finish_kernel,
        grid=(count,),
        in_specs=[
            shifted,
            pl.BlockSpec((1, dom, dom), lambda p: (p, 0, 0)),
            shifted,
            shifted,
        ]
        + [pl.BlockSpec(memory_space=pl.ANY)] * len(extra),
        out_specs=[shifted, shifted],
        out_shape=[shape, shape],
        input_output_aliases={4: 0, 5: 1} if extra else {},
        compiler_params=pltpu.CompilerParams(vmem_limit_bytes=VMEM),
        cost_estimate=pl.CostEstimate(
            flops=count * dom * dom * 5,
            bytes_accessed=count * dom * dom * 18,
            transcendentals=0,
        ),
    )(own, other, amplitudes, inv, *extra)


CHUNKS = ((0, 4), (4, 12), (12, 16))


def local(orbs, ys, integrals, fock_blocks, occ_energy, dom_len, amplitudes, pair_list):
    aux, occ, dom = integrals.shape
    group = occ // orbs
    owned = amplitudes.shape[0]
    y = lax.axis_index("pair")
    even = lax.rem(lax.axis_index("orb"), 2) == 0
    mate = jnp.where(even, 3 - y, y ^ 1)
    pairs = pair_list.reshape(-1)
    mine = (y * owned).reshape(1).astype(jnp.int32)
    theirs = (mate * owned).reshape(1).astype(jnp.int32)
    each = fock_blocks.shape[0]
    number = jnp.arange(group, dtype=jnp.int32)
    slot = ((number // each - y) & 3) * each + number % each
    focks = [fock_blocks] + [
        lax.ppermute(fock_blocks, "pair", [((s + shift) % ys, s) for s in range(ys)])
        for shift in (1, 2, 3)
    ]

    blocks = integrals.reshape(aux, orbs, group, dom).transpose(1, 2, 0, 3)
    near, far = [], []
    for c, (lo, hi) in enumerate(SPLITS):
        block = blocks[:, lo:hi]
        if c == len(SPLITS) - 1:
            block, *focks = lax.optimization_barrier([block] + focks)
        got = lax.all_to_all(block, "orb", split_axis=0, concat_axis=0, tiled=True)
        near.append(got)
        far.append(exchange_with(got, gather_mate, orbs, ys))
    parts = near + far

    others = []
    for lo, hi in CHUNKS:
        sums = partial_sums(parts, pairs, theirs, lo, hi - lo)
        others.append(exchange_with(sums, sum_mate, orbs, ys))
    base, inv = fock_terms(focks, amplitudes, pairs, mine, slot, occ_energy, dom_len)
    own = own_sums(parts, base, pairs, mine)
    held = None
    for (lo, _), other in zip(CHUNKS, others):
        held = finish(own, other, amplitudes, inv, lo, held)
    return tuple(held)


def solution(mesh):
    placed = (
        P(("orb", "pair"), None, None),
        P(("orb", "pair"), None, None),
        P("orb"),
        P("orb"),
        P(("orb", "pair"), None, None),
        P("orb", None),
    )
    return jax.shard_map(
        functools.partial(local, mesh.shape["orb"], mesh.shape["pair"]),
        mesh=mesh,
        in_specs=placed,
        out_specs=(P(("orb", "pair"), None, None), P(("orb", "pair"), None, None)),
        check_vma=False,
    )
```

```python
import functools

import jax
import jax.numpy as jnp
from jax import lax
from jax.experimental import pallas as pl
from jax.experimental.pallas import tpu as pltpu
from jax.sharding import PartitionSpec as P

BOTH = ("orb", "pair")
SPLITS = ((0, 12), (12, 16))
VMEM = 24 * 2**20
ARRANGE = 8
STEPS = 32767.0
TAIL = 16


def gather_mate(orb, y):
    return y ^ 1 if orb % 2 == 0 else 3 - y


def sum_mate(orb, y):
    return 3 - y if orb % 2 == 0 else y ^ 1


def exchange_with(x, mate, orbs, ys):
    pairs = [(o * ys + y, o * ys + mate(o, y)) for o in range(orbs) for y in range(ys)]
    return lax.ppermute(x, BOTH, pairs)


def arrange_kernel(move_ref, x_ref, *out_refs):
    aux, rows, dom = x_ref.shape
    group = SPLITS[-1][1]
    for g in range(rows // group):
        block = x_ref[:, g * group : (g + 1) * group, :].reshape(aux * group, dom)
        moved = jnp.dot(move_ref[...], block, preferred_element_type=jnp.float32)
        moved = moved.astype(x_ref.dtype).reshape(group, aux, dom)
        for (lo, hi), out_ref in zip(SPLITS, out_refs):
            out_ref[g] = moved[lo:hi]


def arrange(integrals, orbs):
    aux, occ, dom = integrals.shape
    group = occ // orbs
    size = aux * group
    new = jnp.arange(size, dtype=jnp.int32)
    source = (new % aux) * group + new // aux
    move = (source[:, None] == new[None, :]).astype(integrals.dtype)
    return pl.pallas_call(
        arrange_kernel,
        grid=(orbs // ARRANGE,),
        in_specs=[
            pl.BlockSpec((size, size), lambda g: (0, 0)),
            pl.BlockSpec((aux, ARRANGE * group, dom), lambda g: (0, g, 0)),
        ],
        out_specs=[
            pl.BlockSpec((ARRANGE, hi - lo, aux, dom), lambda g: (g, 0, 0, 0))
            for lo, hi in SPLITS
        ],
        out_shape=[
            jax.ShapeDtypeStruct((orbs, hi - lo, aux, dom), integrals.dtype)
            for lo, hi in SPLITS
        ],
        compiler_params=pltpu.CompilerParams(vmem_limit_bytes=VMEM),
        cost_estimate=pl.CostEstimate(
            flops=2 * orbs * size * size * dom,
            bytes_accessed=4 * aux * occ * dom,
            transcendentals=0,
        ),
    )(move, integrals)


def load_blocks(parts, held, sems):
    return [
        pltpu.make_async_copy(part, held.at[c // len(SPLITS), :, lo:hi], sems.at[c])
        for c, (part, (lo, hi)) in enumerate(zip(parts, SPLITS * held.shape[0]))
    ]


def block_sum(held, i, j):
    total = None
    for h in range(held.shape[0]):
        left = held[h, :, i].reshape(-1, held.shape[-1])
        right = held[h, :, j].reshape(-1, held.shape[-1])
        term = lax.dot_general(
            left, right, (((0,), (0,)), ((), ())), preferred_element_type=jnp.float32
        )
        total = term if total is None else total + term
    return total


def column_tops(mantissa, power):
    return mantissa.astype(jnp.float32) * jnp.exp2(power.astype(jnp.float32))


def encode(total, out_ref):
    dom = total.shape[0]
    top = jnp.maximum(jnp.max(jnp.abs(total), axis=0, keepdims=True), 1e-30)
    power = jnp.floor(jnp.log2(top)).astype(jnp.int32) - 13
    mantissa = (top * jnp.exp2(-power.astype(jnp.float32))).astype(jnp.int32) + 1
    scale = STEPS / column_tops(mantissa, power)
    out_ref[0, :dom, :] = jnp.round(total * scale).astype(jnp.int32).astype(jnp.int16)
    rows = lax.broadcasted_iota(jnp.int32, (TAIL, total.shape[1]), 0)
    out_ref[0, dom:, :] = jnp.where(rows == 0, mantissa, power).astype(jnp.int16)


def decode(code_ref):
    dom = code_ref.shape[-1]
    tail = code_ref[0, dom:, :].astype(jnp.int32)
    step = column_tops(tail[0:1], tail[1:2]) * (1.0 / STEPS)
    return code_ref[0, :dom, :].astype(jnp.float32) * step


def sums_kernel(rows, added, coded, pairs_ref, begin_ref, *refs):
    held, sems = refs[-2:]
    count = held.shape[0] * len(SPLITS)
    parts, base_refs = refs[:count], refs[count : count + sum(added)]
    out_refs = refs[count + sum(added) : -2]
    p = pl.program_id(0)

    @pl.when(p == 0)
    def _():
        copies = load_blocks(parts, held, sems)
        for c in copies:
            c.start()
        for c in copies:
            c.wait()

    bases = iter(base_refs)
    for k, (first, has) in enumerate(zip(rows, added)):
        row = begin_ref[k] + first + p
        total = block_sum(held, pairs_ref[2 * row], pairs_ref[2 * row + 1])
        if has:
            total += next(bases)[0]
        if coded:
            encode(total, out_refs[k])
        else:
            out_refs[k][0] = total


def pair_sums(parts, bases, pairs, begins, firsts, count, coded=False):
    src, _, aux, dom = parts[0].shape
    orbs = SPLITS[-1][1]
    added = tuple(b is not None for b in bases)
    in_specs = [pl.BlockSpec(memory_space=pl.ANY)] * len(parts) + [
        pl.BlockSpec((1, dom, dom), lambda p, *_, first=first: (p + first, 0, 0))
        for first, has in zip(firsts, added)
        if has
    ]
    shape = (
        jax.ShapeDtypeStruct((count, dom + TAIL, dom), jnp.int16)
        if coded
        else jax.ShapeDtypeStruct((count, dom, dom), jnp.float32)
    )
    return pl.pallas_call(
        functools.partial(sums_kernel, tuple(firsts), added, coded),
        grid_spec=pltpu.PrefetchScalarGridSpec(
            num_scalar_prefetch=2,
            grid=(count,),
            in_specs=in_specs,
            out_specs=[pl.BlockSpec((1,) + shape.shape[1:], lambda p, *_: (p, 0, 0))]
            * len(begins),
            scratch_shapes=[
                pltpu.VMEM((len(parts) // len(SPLITS), src, orbs, aux, dom), jnp.bfloat16),
                pltpu.SemaphoreType.DMA((len(parts),)),
            ],
        ),
        out_shape=[shape] * len(begins),
        compiler_params=pltpu.CompilerParams(vmem_limit_bytes=VMEM),
        cost_estimate=pl.CostEstimate(
            flops=2 * count * len(begins) * src * aux * dom * dom * len(parts) // len(SPLITS),
            bytes_accessed=2 * src * orbs * aux * dom * len(parts) // len(SPLITS)
            + count * dom * dom * 4 * (len(begins) + sum(added)),
            transcendentals=0,
        ),
    )(pairs, jnp.stack(begins), *parts, *[b for b in bases if b is not None])


def fock_kernel(pairs_ref, begin_ref, slot_ref, occ_ref, len_ref, *refs):
    focks, amp_ref, base_ref, inv_ref, fock, sems = refs[:4], refs[4], *refs[5:]
    p = pl.program_id(0)
    dom = fock.shape[-1]

    @pl.when(p == 0)
    def _():
        each = focks[0].shape[0]
        copies = [
            pltpu.make_async_copy(
                focks[s], fock.at[s * each : (s + 1) * each], sems.at[s]
            )
            for s in range(4)
        ]
        for c in copies:
            c.start()
        for c in copies:
            c.wait()

    row = begin_ref[0] + p
    i = pairs_ref[2 * row]
    j = pairs_ref[2 * row + 1]
    energies = occ_ref[i] + occ_ref[j]
    old = amp_ref[0]
    fock_i = fock[slot_ref[i]]
    fock_j = fock[slot_ref[j]]
    total = jnp.dot(fock_i, old, preferred_element_type=jnp.float32)
    total += lax.dot_general(
        old, fock_j, (((1,), (1,)), ((), ())), preferred_element_type=jnp.float32
    )
    base_ref[0] = total - energies * old.astype(jnp.float32)
    rows = lax.broadcasted_iota(jnp.int32, (dom, dom), 0)
    columns = lax.broadcasted_iota(jnp.int32, (dom, dom), 1)
    eye = rows == columns
    diag_i = jnp.sum(
        jnp.where(eye, fock_i.astype(jnp.float32), 0.0), axis=1, keepdims=True
    )
    diag_j = jnp.sum(
        jnp.where(eye, fock_j.astype(jnp.float32), 0.0), axis=0, keepdims=True
    )
    inside = (rows < len_ref[i]) & (columns < len_ref[j])
    inv_ref[0] = jnp.where(inside, 1.0 / (diag_i + diag_j - energies), 0.0)


def fock_terms(focks, amplitudes, pairs, begin, slot, occ, lengths):
    count, dom, _ = amplitudes.shape
    one = pl.BlockSpec((1, dom, dom), lambda p, *_: (p, 0, 0))
    shape = jax.ShapeDtypeStruct((count, dom, dom), jnp.float32)
    return pl.pallas_call(
        fock_kernel,
        grid_spec=pltpu.PrefetchScalarGridSpec(
            num_scalar_prefetch=5,
            grid=(count,),
            in_specs=[pl.BlockSpec(memory_space=pl.ANY)] * 4 + [one],
            out_specs=[one, one],
            scratch_shapes=[
                pltpu.VMEM((4 * focks[0].shape[0], dom, dom), jnp.bfloat16),
                pltpu.SemaphoreType.DMA((4,)),
            ],
        ),
        out_shape=[shape, shape],
        compiler_params=pltpu.CompilerParams(vmem_limit_bytes=VMEM),
        cost_estimate=pl.CostEstimate(
            flops=2 * count * 2 * dom * dom * dom,
            bytes_accessed=count * dom * dom * 12,
            transcendentals=0,
        ),
    )(pairs, begin, slot, occ, lengths, *focks, amplitudes)


def finish_kernel(own_ref, other_ref, amp_ref, inv_ref, *refs):
    resid_ref, new_ref = refs[-2:]
    inv = inv_ref[0]
    inside = inv != 0.0
    resid = jnp.where(inside, own_ref[0] + decode(other_ref), 0.0)
    old = amp_ref[0].astype(jnp.float32)
    resid_ref[0] = resid.astype(resid_ref.dtype)
    new_ref[0] = jnp.where(inside, old - resid * inv, 0.0).astype(new_ref.dtype)


def finish(own, other, amplitudes, inv, first, held):
    total, dom, _ = amplitudes.shape
    count = other.shape[0]
    shifted = pl.BlockSpec((1, dom, dom), lambda p: (p + first, 0, 0))
    shape = jax.ShapeDtypeStruct((total, dom, dom), jnp.bfloat16)
    extra = [] if held is None else list(held)
    return pl.pallas_call(
        finish_kernel,
        grid=(count,),
        in_specs=[
            shifted,
            pl.BlockSpec((1,) + other.shape[1:], lambda p: (p, 0, 0)),
            shifted,
            shifted,
        ]
        + [pl.BlockSpec(memory_space=pl.ANY)] * len(extra),
        out_specs=[shifted, shifted],
        out_shape=[shape, shape],
        input_output_aliases={4: 0, 5: 1} if extra else {},
        compiler_params=pltpu.CompilerParams(vmem_limit_bytes=VMEM),
        cost_estimate=pl.CostEstimate(
            flops=count * dom * dom * 5,
            bytes_accessed=count * dom * dom * 18,
            transcendentals=0,
        ),
    )(own, other, amplitudes, inv, *extra)


CHUNKS = ((0, 6), (6, 11), (11, 16))


def local(orbs, ys, integrals, fock_blocks, occ_energy, dom_len, amplitudes, pair_list):
    aux, occ, dom = integrals.shape
    group = occ // orbs
    owned = amplitudes.shape[0]
    y = lax.axis_index("pair")
    even = lax.rem(lax.axis_index("orb"), 2) == 0
    mate = jnp.where(even, 3 - y, y ^ 1)
    pairs = pair_list.reshape(-1)
    mine = (y * owned).astype(jnp.int32)
    theirs = (mate * owned).astype(jnp.int32)
    each = fock_blocks.shape[0]
    number = jnp.arange(group, dtype=jnp.int32)
    slot = ((number // each - y) & 3) * each + number % each
    focks = [fock_blocks] + [
        lax.ppermute(fock_blocks, "pair", [((s + shift) % ys, s) for s in range(ys)])
        for shift in (1, 2, 3)
    ]

    blocks = arrange(integrals, orbs)
    near, far = [], []
    for c, block in enumerate(blocks):
        if c == len(SPLITS) - 1:
            block, *focks = lax.optimization_barrier([block] + focks)
        got = lax.all_to_all(block, "orb", split_axis=0, concat_axis=0, tiled=True)
        near.append(got)
        far.append(exchange_with(got, gather_mate, orbs, ys))

    base, inv = fock_terms(
        focks, amplitudes, pairs, mine.reshape(1), slot, occ_energy, dom_len
    )
    after, base, inv = lax.optimization_barrier((near[0], base, inv))
    (theirs_near,) = pair_sums([after] + near[1:], [None], pairs, [theirs], [0], owned)
    others = []
    for lo, hi in CHUNKS:
        (sums,) = pair_sums(far, [theirs_near], pairs, [theirs], [lo], hi - lo, True)
        others.append(exchange_with(sums, sum_mate, orbs, ys))
    (own,) = pair_sums(near + far, [base], pairs, [mine], [0], owned)
    held = None
    for (lo, _), other in zip(CHUNKS, others):
        held = finish(own, other, amplitudes, inv, lo, held)
    return tuple(held)


def solution(mesh):
    placed = (
        P(("orb", "pair"), None, None),
        P(("orb", "pair"), None, None),
        P("orb"),
        P("orb"),
        P(("orb", "pair"), None, None),
        P("orb", None),
    )
    return jax.shard_map(
        functools.partial(local, mesh.shape["orb"], mesh.shape["pair"]),
        mesh=mesh,
        in_specs=placed,
        out_specs=(P(("orb", "pair"), None, None), P(("orb", "pair"), None, None)),
        check_vma=False,
    )
```

```python
import functools

import jax
import jax.numpy as jnp
from jax import lax
from jax.experimental import pallas as pl
from jax.experimental.pallas import tpu as pltpu
from jax.sharding import PartitionSpec as P

BOTH = ("orb", "pair")
SPLITS = ((0, 12), (12, 16))
VMEM = 24 * 2**20
WIDE = 58 * 2**20
PIECES = 8
PER = 4
STEPS = 32767.0
TAIL = 16


def gather_mate(orb, y):
    return y ^ 1 if orb % 2 == 0 else 3 - y


def sum_mate(orb, y):
    return 3 - y if orb % 2 == 0 else y ^ 1


def exchange_with(x, mate, orbs, ys):
    pairs = [(o * ys + y, o * ys + mate(o, y)) for o in range(orbs) for y in range(ys)]
    return lax.ppermute(x, BOTH, pairs)


def arrange_kernel(x_ref, *refs):
    n = len(SPLITS)
    out_refs, x, outs, sems, out_sems = refs[:n], refs[n], refs[n + 1 : -2], refs[-2], refs[-1]
    aux, occ, dom = x.shape
    group = SPLITS[-1][1]
    size = aux * group
    each = occ // group // PIECES
    loads = [
        pltpu.make_async_copy(
            x_ref.at[:, k * each * group : (k + 1) * each * group],
            x.at[:, k * each * group : (k + 1) * each * group],
            sems.at[k],
        )
        for k in range(PIECES)
    ]
    for c in loads:
        c.start()
    new = lax.broadcasted_iota(jnp.int32, (size, size), 0)
    old = lax.broadcasted_iota(jnp.int32, (size, size), 1)
    move = jnp.where((new % aux) * group + new // aux == old, 1.0, 0.0).astype(x.dtype)
    stores = []
    for k in range(PIECES):
        loads[k].wait()
        for g in range(k * each, (k + 1) * each):
            block = x[:, g * group : (g + 1) * group, :].reshape(size, dom)
            moved = jnp.dot(move, block, preferred_element_type=jnp.float32)
            moved = moved.astype(x.dtype).reshape(group, aux, dom)
            for (lo, hi), out in zip(SPLITS, outs):
                out[g] = moved[lo:hi]
        for c in range(n):
            store = pltpu.make_async_copy(
                outs[c].at[k * each : (k + 1) * each],
                out_refs[c].at[k * each : (k + 1) * each],
                out_sems.at[c, k],
            )
            store.start()
            stores.append(store)
    for c in stores:
        c.wait()


def arrange(integrals, orbs):
    aux, occ, dom = integrals.shape
    size = aux * (occ // orbs)
    shapes = [(orbs, hi - lo, aux, dom) for lo, hi in SPLITS]
    return pl.pallas_call(
        arrange_kernel,
        in_specs=[pl.BlockSpec(memory_space=pl.ANY)],
        out_specs=[pl.BlockSpec(memory_space=pl.ANY)] * len(shapes),
        out_shape=[jax.ShapeDtypeStruct(v, integrals.dtype) for v in shapes],
        scratch_shapes=[pltpu.VMEM(integrals.shape, integrals.dtype)]
        + [pltpu.VMEM(v, integrals.dtype) for v in shapes]
        + [
            pltpu.SemaphoreType.DMA((PIECES,)),
            pltpu.SemaphoreType.DMA((len(shapes), PIECES)),
        ],
        compiler_params=pltpu.CompilerParams(vmem_limit_bytes=WIDE),
        cost_estimate=pl.CostEstimate(
            flops=2 * orbs * size * size * dom,
            bytes_accessed=4 * aux * occ * dom,
            transcendentals=0,
        ),
    )(integrals)


def load_blocks(parts, held, sems):
    return [
        pltpu.make_async_copy(part, held.at[c // len(SPLITS), :, lo:hi], sems.at[c])
        for c, (part, (lo, hi)) in enumerate(zip(parts, SPLITS * held.shape[0]))
    ]


def block_sum(held, i, j):
    total = None
    for h in range(held.shape[0]):
        left = held[h, :, i].reshape(-1, held.shape[-1])
        right = held[h, :, j].reshape(-1, held.shape[-1])
        term = lax.dot_general(
            left, right, (((0,), (0,)), ((), ())), preferred_element_type=jnp.float32
        )
        total = term if total is None else total + term
    return total


def column_tops(mantissa, power):
    return mantissa.astype(jnp.float32) * jnp.exp2(power.astype(jnp.float32))


def encode(total, out_ref, q):
    dom = total.shape[0]
    top = jnp.maximum(jnp.max(jnp.abs(total), axis=0, keepdims=True), 1e-30)
    power = jnp.floor(jnp.log2(top)).astype(jnp.int32) - 13
    mantissa = (top * jnp.exp2(-power.astype(jnp.float32))).astype(jnp.int32) + 1
    scale = STEPS / column_tops(mantissa, power)
    out_ref[q, :dom, :] = jnp.round(total * scale).astype(jnp.int32).astype(jnp.int16)
    rows = lax.broadcasted_iota(jnp.int32, (TAIL, total.shape[1]), 0)
    out_ref[q, dom:, :] = jnp.where(rows == 0, mantissa, power).astype(jnp.int16)


def decode(code_ref, q):
    dom = code_ref.shape[-1]
    tail = code_ref[q, dom:, :].astype(jnp.int32)
    step = column_tops(tail[0:1], tail[1:2]) * (1.0 / STEPS)
    return code_ref[q, :dom, :].astype(jnp.float32) * step


def sums_kernel(rows, added, coded, pairs_ref, begin_ref, *refs):
    held, sems = refs[-2:]
    count = held.shape[0] * len(SPLITS)
    parts, base_refs = refs[:count], refs[count : count + sum(added)]
    out_refs = refs[count + sum(added) : -2]
    p = pl.program_id(0)

    @pl.when(p == 0)
    def _():
        copies = load_blocks(parts, held, sems)
        for c in copies:
            c.start()
        for c in copies:
            c.wait()

    per = out_refs[0].shape[0]
    for q in range(per):
        bases = iter(base_refs)
        for k, (first, has) in enumerate(zip(rows, added)):
            row = begin_ref[k] + first + p * per + q
            total = block_sum(held, pairs_ref[2 * row], pairs_ref[2 * row + 1])
            if has:
                total += next(bases)[q]
            if coded:
                encode(total, out_refs[k], q)
            else:
                out_refs[k][q] = total


def pair_sums(parts, bases, pairs, begins, firsts, count, coded=False, per=PER):
    src, _, aux, dom = parts[0].shape
    orbs = SPLITS[-1][1]
    added = tuple(b is not None for b in bases)
    in_specs = [pl.BlockSpec(memory_space=pl.ANY)] * len(parts) + [
        pl.BlockSpec((per, dom, dom), lambda p, *_, first=first: (p + first // per, 0, 0))
        for first, has in zip(firsts, added)
        if has
    ]
    shape = (
        jax.ShapeDtypeStruct((count, dom + TAIL, dom), jnp.int16)
        if coded
        else jax.ShapeDtypeStruct((count, dom, dom), jnp.float32)
    )
    return pl.pallas_call(
        functools.partial(sums_kernel, tuple(firsts), added, coded),
        grid_spec=pltpu.PrefetchScalarGridSpec(
            num_scalar_prefetch=2,
            grid=(count // per,),
            in_specs=in_specs,
            out_specs=[pl.BlockSpec((per,) + shape.shape[1:], lambda p, *_: (p, 0, 0))]
            * len(begins),
            scratch_shapes=[
                pltpu.VMEM((len(parts) // len(SPLITS), src, orbs, aux, dom), jnp.bfloat16),
                pltpu.SemaphoreType.DMA((len(parts),)),
            ],
        ),
        out_shape=[shape] * len(begins),
        compiler_params=pltpu.CompilerParams(vmem_limit_bytes=VMEM),
        cost_estimate=pl.CostEstimate(
            flops=2 * count * len(begins) * src * aux * dom * dom * len(parts) // len(SPLITS),
            bytes_accessed=2 * src * orbs * aux * dom * len(parts) // len(SPLITS)
            + count * dom * dom * 4 * (len(begins) + sum(added)),
            transcendentals=0,
        ),
    )(pairs, jnp.stack(begins), *parts, *[b for b in bases if b is not None])


def fock_kernel(pairs_ref, begin_ref, slot_ref, occ_ref, len_ref, *refs):
    focks, amp_ref, base_ref, inv_ref, fock, sems = refs[:4], refs[4], *refs[5:]
    p = pl.program_id(0)
    dom = fock.shape[-1]

    @pl.when(p == 0)
    def _():
        each = focks[0].shape[0]
        copies = [
            pltpu.make_async_copy(
                focks[s], fock.at[s * each : (s + 1) * each], sems.at[s]
            )
            for s in range(4)
        ]
        for c in copies:
            c.start()
        for c in copies:
            c.wait()

    per = amp_ref.shape[0]
    for q in range(per):
        row = begin_ref[0] + p * per + q
        i = pairs_ref[2 * row]
        j = pairs_ref[2 * row + 1]
        energies = occ_ref[i] + occ_ref[j]
        old = amp_ref[q]
        fock_i = fock[slot_ref[i]]
        fock_j = fock[slot_ref[j]]
        total = jnp.dot(fock_i, old, preferred_element_type=jnp.float32)
        total += lax.dot_general(
            old, fock_j, (((1,), (1,)), ((), ())), preferred_element_type=jnp.float32
        )
        base_ref[q] = total - energies * old.astype(jnp.float32)
        rows = lax.broadcasted_iota(jnp.int32, (dom, dom), 0)
        columns = lax.broadcasted_iota(jnp.int32, (dom, dom), 1)
        eye = rows == columns
        diag_i = jnp.sum(
            jnp.where(eye, fock_i.astype(jnp.float32), 0.0), axis=1, keepdims=True
        )
        diag_j = jnp.sum(
            jnp.where(eye, fock_j.astype(jnp.float32), 0.0), axis=0, keepdims=True
        )
        inside = (rows < len_ref[i]) & (columns < len_ref[j])
        inv_ref[q] = jnp.where(inside, 1.0 / (diag_i + diag_j - energies), 0.0)


def fock_terms(focks, amplitudes, pairs, begin, slot, occ, lengths):
    count, dom, _ = amplitudes.shape
    one = pl.BlockSpec((PER, dom, dom), lambda p, *_: (p, 0, 0))
    shape = jax.ShapeDtypeStruct((count, dom, dom), jnp.float32)
    return pl.pallas_call(
        fock_kernel,
        grid_spec=pltpu.PrefetchScalarGridSpec(
            num_scalar_prefetch=5,
            grid=(count // PER,),
            in_specs=[pl.BlockSpec(memory_space=pl.ANY)] * 4 + [one],
            out_specs=[one, one],
            scratch_shapes=[
                pltpu.VMEM((4 * focks[0].shape[0], dom, dom), jnp.bfloat16),
                pltpu.SemaphoreType.DMA((4,)),
            ],
        ),
        out_shape=[shape, shape],
        compiler_params=pltpu.CompilerParams(vmem_limit_bytes=VMEM),
        cost_estimate=pl.CostEstimate(
            flops=2 * count * 2 * dom * dom * dom,
            bytes_accessed=count * dom * dom * 12,
            transcendentals=0,
        ),
    )(pairs, begin, slot, occ, lengths, *focks, amplitudes)


def finish_kernel(own_ref, other_ref, amp_ref, inv_ref, *refs):
    resid_ref, new_ref = refs[-2:]
    for q in range(own_ref.shape[0]):
        inv = inv_ref[q]
        inside = inv != 0.0
        resid = jnp.where(inside, own_ref[q] + decode(other_ref, q), 0.0)
        old = amp_ref[q].astype(jnp.float32)
        resid_ref[q] = resid.astype(resid_ref.dtype)
        new_ref[q] = jnp.where(inside, old - resid * inv, 0.0).astype(new_ref.dtype)


def finish(own, other, amplitudes, inv, first, held):
    total, dom, _ = amplitudes.shape
    count = other.shape[0]
    shifted = pl.BlockSpec((PER, dom, dom), lambda p: (p + first // PER, 0, 0))
    shape = jax.ShapeDtypeStruct((total, dom, dom), jnp.bfloat16)
    extra = [] if held is None else list(held)
    return pl.pallas_call(
        finish_kernel,
        grid=(count // PER,),
        in_specs=[
            shifted,
            pl.BlockSpec((PER,) + other.shape[1:], lambda p: (p, 0, 0)),
            shifted,
            shifted,
        ]
        + [pl.BlockSpec(memory_space=pl.ANY)] * len(extra),
        out_specs=[shifted, shifted],
        out_shape=[shape, shape],
        input_output_aliases={4: 0, 5: 1} if extra else {},
        compiler_params=pltpu.CompilerParams(vmem_limit_bytes=VMEM),
        cost_estimate=pl.CostEstimate(
            flops=count * dom * dom * 5,
            bytes_accessed=count * dom * dom * 18,
            transcendentals=0,
        ),
    )(own, other, amplitudes, inv, *extra)


CHUNKS = ((0, 4), (4, 8), (8, 12), (12, 16))


def local(orbs, ys, integrals, fock_blocks, occ_energy, dom_len, amplitudes, pair_list):
    aux, occ, dom = integrals.shape
    group = occ // orbs
    owned = amplitudes.shape[0]
    y = lax.axis_index("pair")
    even = lax.rem(lax.axis_index("orb"), 2) == 0
    mate = jnp.where(even, 3 - y, y ^ 1)
    pairs = pair_list.reshape(-1)
    mine = (y * owned).astype(jnp.int32)
    theirs = (mate * owned).astype(jnp.int32)
    each = fock_blocks.shape[0]
    number = jnp.arange(group, dtype=jnp.int32)
    slot = ((number // each - y) & 3) * each + number % each
    focks = [fock_blocks] + [
        lax.ppermute(fock_blocks, "pair", [((s + shift) % ys, s) for s in range(ys)])
        for shift in (1, 2, 3)
    ]

    blocks = arrange(integrals, orbs)
    near, far = [], []
    for c, block in enumerate(blocks):
        if c == len(SPLITS) - 1:
            block, *focks = lax.optimization_barrier([block] + focks)
            base, inv = fock_terms(
                focks, amplitudes, pairs, mine.reshape(1), slot, occ_energy, dom_len
            )
        got = lax.all_to_all(block, "orb", split_axis=0, concat_axis=0, tiled=True)
        if c == len(SPLITS) - 1:
            got, base, inv = lax.optimization_barrier((got, base, inv))
        near.append(got)
        far.append(exchange_with(got, gather_mate, orbs, ys))

    theirs_near, own = pair_sums(near, [None, base], pairs, [theirs, mine], [0, 0], owned)
    others = []
    for lo, hi in CHUNKS:
        (sums,) = pair_sums(far, [theirs_near], pairs, [theirs], [lo], hi - lo, True)
        others.append(exchange_with(sums, sum_mate, orbs, ys))
    (own,) = pair_sums(far, [own], pairs, [mine], [0], owned)
    held = None
    for (lo, _), other in zip(CHUNKS, others):
        held = finish(own, other, amplitudes, inv, lo, held)
    return tuple(held)


def solution(mesh):
    placed = (
        P(("orb", "pair"), None, None),
        P(("orb", "pair"), None, None),
        P("orb"),
        P("orb"),
        P(("orb", "pair"), None, None),
        P("orb", None),
    )
    return jax.shard_map(
        functools.partial(local, mesh.shape["orb"], mesh.shape["pair"]),
        mesh=mesh,
        in_specs=placed,
        out_specs=(P(("orb", "pair"), None, None), P(("orb", "pair"), None, None)),
        check_vma=False,
    )
```

```python
import functools
import math

import jax
import jax.numpy as jnp
from jax import lax
from jax.experimental import pallas as pl
from jax.experimental.pallas import tpu as pltpu
from jax.sharding import PartitionSpec as P

BOTH = ("orb", "pair")
SPLITS = ((0, 12), (12, 16))
VMEM = 24 * 2**20
WIDE = 58 * 2**20
PIECES = 4
PER = 4
STEPS = 32767.0
TAIL = 16


def gather_mate(orb, y):
    return y ^ 1 if orb % 2 == 0 else 3 - y


def sum_mate(orb, y):
    return 3 - y if orb % 2 == 0 else y ^ 1


def exchange_with(x, mate, orbs, ys):
    pairs = [(o * ys + y, o * ys + mate(o, y)) for o in range(orbs) for y in range(ys)]
    return lax.ppermute(x, BOTH, pairs)


def arrange_kernel(lo, hi, x_ref, out_ref, x, out, sems, out_sems):
    aux, occ, dom = x.shape
    group = SPLITS[-1][1]
    each = occ // group // PIECES
    loads = [
        pltpu.make_async_copy(
            x_ref.at[:, k * each * group : (k + 1) * each * group],
            x.at[:, k * each * group : (k + 1) * each * group],
            sems.at[k],
        )
        for k in range(PIECES)
    ]
    for c in loads:
        c.start()
    size = ((hi - lo) * aux, aux * group)
    new = lax.broadcasted_iota(jnp.int32, size, 0)
    old = lax.broadcasted_iota(jnp.int32, size, 1)
    move = jnp.where((new % aux) * group + new // aux + lo == old, 1.0, 0.0).astype(x.dtype)
    stores = []
    for k in range(PIECES):
        loads[k].wait()
        for g in range(k * each, (k + 1) * each):
            block = x[:, g * group : (g + 1) * group, :].reshape(aux * group, dom)
            moved = jnp.dot(move, block, preferred_element_type=jnp.float32)
            out[g] = moved.astype(x.dtype).reshape(hi - lo, aux, dom)
        store = pltpu.make_async_copy(
            out.at[k * each : (k + 1) * each],
            out_ref.at[k * each : (k + 1) * each],
            out_sems.at[k],
        )
        store.start()
        stores.append(store)
    for c in stores:
        c.wait()


def arrange(integrals, orbs, lo, hi):
    aux, occ, dom = integrals.shape
    shape = (orbs, hi - lo, aux, dom)
    return pl.pallas_call(
        functools.partial(arrange_kernel, lo, hi),
        in_specs=[pl.BlockSpec(memory_space=pl.ANY)],
        out_specs=pl.BlockSpec(memory_space=pl.ANY),
        out_shape=jax.ShapeDtypeStruct(shape, integrals.dtype),
        scratch_shapes=[
            pltpu.VMEM(integrals.shape, integrals.dtype),
            pltpu.VMEM(shape, integrals.dtype),
            pltpu.SemaphoreType.DMA((PIECES,)),
            pltpu.SemaphoreType.DMA((PIECES,)),
        ],
        compiler_params=pltpu.CompilerParams(vmem_limit_bytes=WIDE),
        cost_estimate=pl.CostEstimate(
            flops=2 * orbs * (hi - lo) * aux * aux * (occ // orbs) * dom,
            bytes_accessed=2 * aux * occ * dom,
            transcendentals=0,
        ),
    )(integrals)


def load_blocks(parts, held, sems):
    return [
        pltpu.make_async_copy(part, held.at[c // len(SPLITS), :, lo:hi], sems.at[c])
        for c, (part, (lo, hi)) in enumerate(zip(parts, SPLITS * held.shape[0]))
    ]


def block_sum(held, i, j):
    total = None
    for h in range(held.shape[0]):
        left = held[h, :, i].reshape(-1, held.shape[-1])
        right = held[h, :, j].reshape(-1, held.shape[-1])
        term = lax.dot_general(
            left, right, (((0,), (0,)), ((), ())), preferred_element_type=jnp.float32
        )
        total = term if total is None else total + term
    return total


def column_tops(mantissa, power):
    return mantissa.astype(jnp.float32) * jnp.exp2(power.astype(jnp.float32))


def encode(totals, out_ref):
    dom = out_ref.shape[1]
    rows = lax.broadcasted_iota(jnp.int32, (TAIL, dom), 0)
    sizes = jnp.zeros((TAIL, dom), jnp.int32)
    for q, total in enumerate(totals):
        top = jnp.maximum(jnp.max(jnp.abs(total), axis=0, keepdims=True), 1e-30)
        power = jnp.floor(jnp.log2(top)).astype(jnp.int32) - 13
        mantissa = (top * jnp.exp2(-power.astype(jnp.float32))).astype(jnp.int32) + 1
        steps = jnp.round(total * (STEPS / column_tops(mantissa, power)))
        out_ref[q * dom : (q + 1) * dom, :] = steps.astype(jnp.int32).astype(jnp.int16)
        sizes = jnp.where(rows == 2 * q, mantissa, sizes)
        sizes = jnp.where(rows == 2 * q + 1, power, sizes)
    out_ref[len(totals) * dom :, :] = sizes.astype(jnp.int16)


def decode(code_ref, q):
    dom = code_ref.shape[1]
    rows = lax.broadcasted_iota(jnp.int32, (TAIL, dom), 0)
    sizes = code_ref[code_ref.shape[0] - TAIL :, :].astype(jnp.int32)
    mantissa = jnp.sum(jnp.where(rows == 2 * q, sizes, 0), axis=0, keepdims=True)
    power = jnp.sum(jnp.where(rows == 2 * q + 1, sizes, 0), axis=0, keepdims=True)
    start = pl.multiple_of(q * dom, dom)
    steps = code_ref[pl.ds(start, dom), :].astype(jnp.int32).astype(jnp.float32)
    return steps * (column_tops(mantissa, power) * (1.0 / STEPS))


def send_kernel(first, pairs_ref, begin_ref, *refs):
    parts, base_ref, out_ref, held, base, sems, base_sem = refs[:2], *refs[2:]
    count = base.shape[0]
    cut = SPLITS[0][1]
    whole = pltpu.make_async_copy(base_ref.at[first : first + count], base, base_sem)
    for q in range(count):
        row = begin_ref[0] + first + q
        for side in range(2):
            k = pairs_ref[2 * row + side]

            @pl.when(k < cut)
            def _():
                pltpu.make_async_copy(
                    parts[0].at[:, k], held.at[q, side], sems.at[q, side]
                ).start()

            @pl.when(k >= cut)
            def _():
                pltpu.make_async_copy(
                    parts[1].at[:, k - cut], held.at[q, side], sems.at[q, side]
                ).start()

        if q == 0:
            whole.start()
    totals = []
    for q in range(count):
        for side in range(2):
            pltpu.make_async_copy(
                parts[0].at[:, 0], held.at[q, side], sems.at[q, side]
            ).wait()
        if q == 0:
            whole.wait()
        left = held[q, 0].reshape(-1, held.shape[-1])
        right = held[q, 1].reshape(-1, held.shape[-1])
        term = lax.dot_general(
            left, right, (((0,), (0,)), ((), ())), preferred_element_type=jnp.float32
        )
        totals.append(base[q] + term)
    encode(totals, out_ref)


def send_sums(parts, base, pairs, begin, first, count):
    src, _, aux, dom = parts[0].shape
    return pl.pallas_call(
        functools.partial(send_kernel, first),
        in_specs=[pl.BlockSpec(memory_space=pltpu.SMEM)] * 2
        + [pl.BlockSpec(memory_space=pl.ANY)] * 3,
        out_specs=pl.BlockSpec(memory_space=pltpu.VMEM),
        out_shape=jax.ShapeDtypeStruct((count * dom + TAIL, dom), jnp.int16),
        scratch_shapes=[
            pltpu.VMEM((count, 2, src, aux, dom), jnp.bfloat16),
            pltpu.VMEM((count, dom, dom), jnp.float32),
            pltpu.SemaphoreType.DMA((count, 2)),
            pltpu.SemaphoreType.DMA,
        ],
        compiler_params=pltpu.CompilerParams(vmem_limit_bytes=VMEM),
        cost_estimate=pl.CostEstimate(
            flops=2 * count * src * aux * dom * dom,
            bytes_accessed=count * (4 * src * aux * dom + dom * dom * 6),
            transcendentals=0,
        ),
    )(pairs, begin.reshape(1), *parts, base)


def sums_kernel(rows, added, pairs_ref, begin_ref, *refs):
    held, sems = refs[-2:]
    count = held.shape[0] * len(SPLITS)
    parts, base_refs = refs[:count], refs[count : count + sum(added)]
    out_refs = refs[count + sum(added) : -2]
    p = pl.program_id(0)

    @pl.when(p == 0)
    def _():
        copies = load_blocks(parts, held, sems)
        for c in copies:
            c.start()
        for c in copies:
            c.wait()

    per = out_refs[0].shape[0]
    for q in range(per):
        bases = iter(base_refs)
        for k, (first, has) in enumerate(zip(rows, added)):
            row = begin_ref[k] + first + p * per + q
            total = block_sum(held, pairs_ref[2 * row], pairs_ref[2 * row + 1])
            if has:
                total += next(bases)[q]
            out_refs[k][q] = total


def pair_sums(parts, bases, pairs, begins, firsts, count, per=PER):
    src, _, aux, dom = parts[0].shape
    orbs = SPLITS[-1][1]
    added = tuple(b is not None for b in bases)
    in_specs = [pl.BlockSpec(memory_space=pl.ANY)] * len(parts) + [
        pl.BlockSpec((per, dom, dom), lambda p, *_, first=first: (p + first // per, 0, 0))
        for first, has in zip(firsts, added)
        if has
    ]
    shape = jax.ShapeDtypeStruct((count, dom, dom), jnp.float32)
    return pl.pallas_call(
        functools.partial(sums_kernel, tuple(firsts), added),
        grid_spec=pltpu.PrefetchScalarGridSpec(
            num_scalar_prefetch=2,
            grid=(count // per,),
            in_specs=in_specs,
            out_specs=[pl.BlockSpec((per,) + shape.shape[1:], lambda p, *_: (p, 0, 0))]
            * len(begins),
            scratch_shapes=[
                pltpu.VMEM((len(parts) // len(SPLITS), src, orbs, aux, dom), jnp.bfloat16),
                pltpu.SemaphoreType.DMA((len(parts),)),
            ],
        ),
        out_shape=[shape] * len(begins),
        compiler_params=pltpu.CompilerParams(vmem_limit_bytes=VMEM),
        cost_estimate=pl.CostEstimate(
            flops=2 * count * len(begins) * src * aux * dom * dom * len(parts) // len(SPLITS),
            bytes_accessed=2 * src * orbs * aux * dom * len(parts) // len(SPLITS)
            + count * dom * dom * 4 * (len(begins) + sum(added)),
            transcendentals=0,
        ),
    )(pairs, jnp.stack(begins), *parts, *[b for b in bases if b is not None])


def fock_kernel(pairs_ref, begin_ref, slot_ref, occ_ref, len_ref, *refs):
    focks, amp_ref, base_ref, inv_ref, fock, sems = refs[:4], refs[4], *refs[5:]
    p = pl.program_id(0)
    dom = fock.shape[-1]

    @pl.when(p == 0)
    def _():
        each = focks[0].shape[0]
        copies = [
            pltpu.make_async_copy(
                focks[s], fock.at[s * each : (s + 1) * each], sems.at[s]
            )
            for s in range(4)
        ]
        for c in copies:
            c.start()
        for c in copies:
            c.wait()

    per = amp_ref.shape[0]
    for q in range(per):
        row = begin_ref[0] + p * per + q
        i = pairs_ref[2 * row]
        j = pairs_ref[2 * row + 1]
        energies = occ_ref[i] + occ_ref[j]
        old = amp_ref[q]
        fock_i = fock[slot_ref[i]]
        fock_j = fock[slot_ref[j]]
        total = jnp.dot(fock_i, old, preferred_element_type=jnp.float32)
        total += lax.dot_general(
            old, fock_j, (((1,), (1,)), ((), ())), preferred_element_type=jnp.float32
        )
        base_ref[q] = total - energies * old.astype(jnp.float32)
        rows = lax.broadcasted_iota(jnp.int32, (dom, dom), 0)
        columns = lax.broadcasted_iota(jnp.int32, (dom, dom), 1)
        eye = rows == columns
        diag_i = jnp.sum(
            jnp.where(eye, fock_i.astype(jnp.float32), 0.0), axis=1, keepdims=True
        )
        diag_j = jnp.sum(
            jnp.where(eye, fock_j.astype(jnp.float32), 0.0), axis=0, keepdims=True
        )
        inside = (rows < len_ref[i]) & (columns < len_ref[j])
        inv_ref[q] = jnp.where(inside, 1.0 / (diag_i + diag_j - energies), 0.0)


def fock_terms(focks, amplitudes, pairs, begin, slot, occ, lengths):
    count, dom, _ = amplitudes.shape
    one = pl.BlockSpec((PER, dom, dom), lambda p, *_: (p, 0, 0))
    shape = jax.ShapeDtypeStruct((count, dom, dom), jnp.float32)
    return pl.pallas_call(
        fock_kernel,
        grid_spec=pltpu.PrefetchScalarGridSpec(
            num_scalar_prefetch=5,
            grid=(count // PER,),
            in_specs=[pl.BlockSpec(memory_space=pl.ANY)] * 4 + [one],
            out_specs=[one, one],
            scratch_shapes=[
                pltpu.VMEM((4 * focks[0].shape[0], dom, dom), jnp.bfloat16),
                pltpu.SemaphoreType.DMA((4,)),
            ],
        ),
        out_shape=[shape, shape],
        compiler_params=pltpu.CompilerParams(vmem_limit_bytes=VMEM),
        cost_estimate=pl.CostEstimate(
            flops=2 * count * 2 * dom * dom * dom,
            bytes_accessed=count * dom * dom * 12,
            transcendentals=0,
        ),
    )(pairs, begin, slot, occ, lengths, *focks, amplitudes)


def finish_kernel(own_ref, other_ref, amp_ref, inv_ref, *refs):
    resid_ref, new_ref = refs[-2:]
    per = own_ref.shape[0]
    p = pl.program_id(0)
    for q in range(per):
        inv = inv_ref[q]
        inside = inv != 0.0
        resid = jnp.where(inside, own_ref[q] + decode(other_ref, p * per + q), 0.0)
        old = amp_ref[q].astype(jnp.float32)
        resid_ref[q] = resid.astype(resid_ref.dtype)
        new_ref[q] = jnp.where(inside, old - resid * inv, 0.0).astype(new_ref.dtype)


def finish(own, other, amplitudes, inv, first, held):
    total, dom, _ = amplitudes.shape
    count = (other.shape[0] - TAIL) // dom
    per = math.gcd(first, count)
    shifted = pl.BlockSpec((per, dom, dom), lambda p: (p + first // per, 0, 0))
    shape = jax.ShapeDtypeStruct((total, dom, dom), jnp.bfloat16)
    extra = [] if held is None else list(held)
    return pl.pallas_call(
        finish_kernel,
        grid=(count // per,),
        in_specs=[
            shifted,
            pl.BlockSpec(other.shape, lambda p: (0, 0)),
            shifted,
            shifted,
        ]
        + [pl.BlockSpec(memory_space=pl.ANY)] * len(extra),
        out_specs=[shifted, shifted],
        out_shape=[shape, shape],
        input_output_aliases={4: 0, 5: 1} if extra else {},
        compiler_params=pltpu.CompilerParams(vmem_limit_bytes=VMEM),
        cost_estimate=pl.CostEstimate(
            flops=count * dom * dom * 5,
            bytes_accessed=count * dom * dom * 18,
            transcendentals=0,
        ),
    )(own, other, amplitudes, inv, *extra)


CHUNKS = ((0, 4), (4, 8), (8, 12), (12, 16))


def local(orbs, ys, integrals, fock_blocks, occ_energy, dom_len, amplitudes, pair_list):
    aux, occ, dom = integrals.shape
    group = occ // orbs
    owned = amplitudes.shape[0]
    y = lax.axis_index("pair")
    even = lax.rem(lax.axis_index("orb"), 2) == 0
    mate = jnp.where(even, 3 - y, y ^ 1)
    pairs = pair_list.reshape(-1)
    mine = (y * owned).astype(jnp.int32)
    theirs = (mate * owned).astype(jnp.int32)
    each = fock_blocks.shape[0]
    number = jnp.arange(group, dtype=jnp.int32)
    slot = ((number // each - y) & 3) * each + number % each
    focks = [fock_blocks] + [
        lax.ppermute(fock_blocks, "pair", [((s + shift) % ys, s) for s in range(ys)])
        for shift in (1, 2, 3)
    ]

    blocks = [arrange(integrals, orbs, lo, hi) for lo, hi in SPLITS]
    near, far = [], []
    for c in range(len(SPLITS)):
        block = blocks[c]
        if c == len(SPLITS) - 1:
            block, *focks = lax.optimization_barrier([block] + focks)
            base, inv = fock_terms(
                focks, amplitudes, pairs, mine.reshape(1), slot, occ_energy, dom_len
            )
        got = lax.all_to_all(block, "orb", split_axis=0, concat_axis=0, tiled=True)
        if c == 0:
            got, blocks[1] = lax.optimization_barrier((got, blocks[1]))
        if c == len(SPLITS) - 1:
            got, base, inv = lax.optimization_barrier((got, base, inv))
        near.append(got)
        far.append(exchange_with(got, gather_mate, orbs, ys))

    theirs_near, own = pair_sums(near, [None, base], pairs, [theirs, mine], [0, 0], owned)
    others = []
    for lo, hi in CHUNKS:
        sums = send_sums(far, theirs_near, pairs, theirs, lo, hi - lo)
        others.append(exchange_with(sums, sum_mate, orbs, ys))
    (own,) = pair_sums(far, [own], pairs, [mine], [0], owned)
    held = None
    for (lo, _), other in zip(CHUNKS, others):
        held = finish(own, other, amplitudes, inv, lo, held)
    return tuple(held)


def solution(mesh):
    placed = (
        P(("orb", "pair"), None, None),
        P(("orb", "pair"), None, None),
        P("orb"),
        P("orb"),
        P(("orb", "pair"), None, None),
        P("orb", None),
    )
    return jax.shard_map(
        functools.partial(local, mesh.shape["orb"], mesh.shape["pair"]),
        mesh=mesh,
        in_specs=placed,
        out_specs=(P(("orb", "pair"), None, None), P(("orb", "pair"), None, None)),
        check_vma=False,
    )
```

```python
import functools
import math

import jax
import jax.numpy as jnp
from jax import lax
from jax.experimental import pallas as pl
from jax.experimental.pallas import tpu as pltpu
from jax.sharding import PartitionSpec as P

BOTH = ("orb", "pair")
SPLITS = ((0, 12), (12, 16))
VMEM = 24 * 2**20
WIDE = 58 * 2**20
PIECES = 4
PER = 4
STEPS = 32767.0
TAIL = 16


def gather_mate(orb, y):
    return y ^ 1 if orb % 2 == 0 else 3 - y


def sum_mate(orb, y):
    return 3 - y if orb % 2 == 0 else y ^ 1


def exchange_with(x, mate, orbs, ys):
    pairs = [(o * ys + y, o * ys + mate(o, y)) for o in range(orbs) for y in range(ys)]
    return lax.ppermute(x, BOTH, pairs)


def arrange_kernel(lo, hi, x_ref, out_ref, x, out, sems, out_sems):
    aux, occ, dom = x.shape
    group = SPLITS[-1][1]
    each = occ // group // PIECES
    loads = [
        pltpu.make_async_copy(
            x_ref.at[:, k * each * group : (k + 1) * each * group],
            x.at[:, k * each * group : (k + 1) * each * group],
            sems.at[k],
        )
        for k in range(PIECES)
    ]
    for c in loads:
        c.start()
    size = ((hi - lo) * aux, aux * group)
    new = lax.broadcasted_iota(jnp.int32, size, 0)
    old = lax.broadcasted_iota(jnp.int32, size, 1)
    move = jnp.where((new % aux) * group + new // aux + lo == old, 1.0, 0.0).astype(x.dtype)
    stores = []
    for k in range(PIECES):
        loads[k].wait()
        for g in range(k * each, (k + 1) * each):
            block = x[:, g * group : (g + 1) * group, :].reshape(aux * group, dom)
            moved = jnp.dot(move, block, preferred_element_type=jnp.float32)
            out[g] = moved.astype(x.dtype).reshape(hi - lo, aux, dom)
        store = pltpu.make_async_copy(
            out.at[k * each : (k + 1) * each],
            out_ref.at[k * each : (k + 1) * each],
            out_sems.at[k],
        )
        store.start()
        stores.append(store)
    for c in stores:
        c.wait()


def arrange(integrals, orbs, lo, hi):
    aux, occ, dom = integrals.shape
    shape = (orbs, hi - lo, aux, dom)
    return pl.pallas_call(
        functools.partial(arrange_kernel, lo, hi),
        in_specs=[pl.BlockSpec(memory_space=pl.ANY)],
        out_specs=pl.BlockSpec(memory_space=pl.ANY),
        out_shape=jax.ShapeDtypeStruct(shape, integrals.dtype),
        scratch_shapes=[
            pltpu.VMEM(integrals.shape, integrals.dtype),
            pltpu.VMEM(shape, integrals.dtype),
            pltpu.SemaphoreType.DMA((PIECES,)),
            pltpu.SemaphoreType.DMA((PIECES,)),
        ],
        compiler_params=pltpu.CompilerParams(vmem_limit_bytes=WIDE),
        cost_estimate=pl.CostEstimate(
            flops=2 * orbs * (hi - lo) * aux * aux * (occ // orbs) * dom,
            bytes_accessed=2 * aux * occ * dom,
            transcendentals=0,
        ),
    )(integrals)


def load_blocks(parts, held, sems):
    return [
        pltpu.make_async_copy(part, held.at[c // len(SPLITS), :, lo:hi], sems.at[c])
        for c, (part, (lo, hi)) in enumerate(zip(parts, SPLITS * held.shape[0]))
    ]


def block_sum(held, i, j):
    total = None
    for h in range(held.shape[0]):
        left = held[h, :, i].reshape(-1, held.shape[-1])
        right = held[h, :, j].reshape(-1, held.shape[-1])
        term = lax.dot_general(
            left, right, (((0,), (0,)), ((), ())), preferred_element_type=jnp.float32
        )
        total = term if total is None else total + term
    return total


def column_tops(mantissa, power):
    return mantissa.astype(jnp.float32) * jnp.exp2(power.astype(jnp.float32))


def encode(totals, out_ref):
    dom = out_ref.shape[1]
    rows = lax.broadcasted_iota(jnp.int32, (TAIL, dom), 0)
    sizes = jnp.zeros((TAIL, dom), jnp.int32)
    for q, total in enumerate(totals):
        top = jnp.maximum(jnp.max(jnp.abs(total), axis=0, keepdims=True), 1e-30)
        power = jnp.floor(jnp.log2(top)).astype(jnp.int32) - 13
        mantissa = (top * jnp.exp2(-power.astype(jnp.float32))).astype(jnp.int32) + 1
        steps = jnp.round(total * (STEPS / column_tops(mantissa, power)))
        out_ref[q * dom : (q + 1) * dom, :] = steps.astype(jnp.int32).astype(jnp.int16)
        sizes = jnp.where(rows == 2 * q, mantissa, sizes)
        sizes = jnp.where(rows == 2 * q + 1, power, sizes)
    out_ref[len(totals) * dom :, :] = sizes.astype(jnp.int16)


def decode(code_ref, q):
    dom = code_ref.shape[1]
    rows = lax.broadcasted_iota(jnp.int32, (TAIL, dom), 0)
    sizes = code_ref[code_ref.shape[0] - TAIL :, :].astype(jnp.int32)
    mantissa = jnp.sum(jnp.where(rows == 2 * q, sizes, 0), axis=0, keepdims=True)
    power = jnp.sum(jnp.where(rows == 2 * q + 1, sizes, 0), axis=0, keepdims=True)
    start = pl.multiple_of(q * dom, dom)
    steps = code_ref[pl.ds(start, dom), :].astype(jnp.int32).astype(jnp.float32)
    return steps * (column_tops(mantissa, power) * (1.0 / STEPS))


def send_kernel(first, pairs_ref, begin_ref, *refs):
    parts, base_ref, out_ref, held, base, sems, base_sem = refs[:2], *refs[2:]
    count = base.shape[0]
    cut = SPLITS[0][1]
    whole = pltpu.make_async_copy(base_ref.at[first : first + count], base, base_sem)
    for q in range(count):
        row = begin_ref[0] + first + q
        for side in range(2):
            k = pairs_ref[2 * row + side]

            @pl.when(k < cut)
            def _():
                pltpu.make_async_copy(
                    parts[0].at[:, k], held.at[q, side], sems.at[q, side]
                ).start()

            @pl.when(k >= cut)
            def _():
                pltpu.make_async_copy(
                    parts[1].at[:, k - cut], held.at[q, side], sems.at[q, side]
                ).start()

        if q == 0:
            whole.start()
    totals = []
    for q in range(count):
        for side in range(2):
            pltpu.make_async_copy(
                parts[0].at[:, 0], held.at[q, side], sems.at[q, side]
            ).wait()
        if q == 0:
            whole.wait()
        left = held[q, 0].reshape(-1, held.shape[-1])
        right = held[q, 1].reshape(-1, held.shape[-1])
        term = lax.dot_general(
            left, right, (((0,), (0,)), ((), ())), preferred_element_type=jnp.float32
        )
        totals.append(base[q] + term)
    encode(totals, out_ref)


def send_sums(parts, base, pairs, begin, first, count):
    src, _, aux, dom = parts[0].shape
    return pl.pallas_call(
        functools.partial(send_kernel, first),
        in_specs=[pl.BlockSpec(memory_space=pltpu.SMEM)] * 2
        + [pl.BlockSpec(memory_space=pl.ANY)] * 3,
        out_specs=pl.BlockSpec(memory_space=pltpu.VMEM),
        out_shape=jax.ShapeDtypeStruct((count * dom + TAIL, dom), jnp.int16),
        scratch_shapes=[
            pltpu.VMEM((count, 2, src, aux, dom), jnp.bfloat16),
            pltpu.VMEM((count, dom, dom), jnp.float32),
            pltpu.SemaphoreType.DMA((count, 2)),
            pltpu.SemaphoreType.DMA,
        ],
        compiler_params=pltpu.CompilerParams(vmem_limit_bytes=VMEM),
        cost_estimate=pl.CostEstimate(
            flops=2 * count * src * aux * dom * dom,
            bytes_accessed=count * (4 * src * aux * dom + dom * dom * 6),
            transcendentals=0,
        ),
    )(pairs, begin.reshape(1), *parts, base)


def sums_kernel(rows, added, pairs_ref, begin_ref, *refs):
    held, sems = refs[-2:]
    count = held.shape[0] * len(SPLITS)
    parts, base_refs = refs[:count], refs[count : count + sum(added)]
    out_refs = refs[count + sum(added) : -2]
    p = pl.program_id(0)

    @pl.when(p == 0)
    def _():
        copies = load_blocks(parts, held, sems)
        for c in copies:
            c.start()
        for c in copies:
            c.wait()

    per = out_refs[0].shape[0]
    for q in range(per):
        bases = iter(base_refs)
        for k, (first, has) in enumerate(zip(rows, added)):
            row = begin_ref[k] + first + p * per + q
            total = block_sum(held, pairs_ref[2 * row], pairs_ref[2 * row + 1])
            if has:
                total += next(bases)[q]
            out_refs[k][q] = total


def pair_sums(parts, bases, pairs, begins, firsts, count, per=PER):
    src, _, aux, dom = parts[0].shape
    orbs = SPLITS[-1][1]
    added = tuple(b is not None for b in bases)
    in_specs = [pl.BlockSpec(memory_space=pl.ANY)] * len(parts) + [
        pl.BlockSpec((per, dom, dom), lambda p, *_, first=first: (p + first // per, 0, 0))
        for first, has in zip(firsts, added)
        if has
    ]
    shape = jax.ShapeDtypeStruct((count, dom, dom), jnp.float32)
    return pl.pallas_call(
        functools.partial(sums_kernel, tuple(firsts), added),
        grid_spec=pltpu.PrefetchScalarGridSpec(
            num_scalar_prefetch=2,
            grid=(count // per,),
            in_specs=in_specs,
            out_specs=[pl.BlockSpec((per,) + shape.shape[1:], lambda p, *_: (p, 0, 0))]
            * len(begins),
            scratch_shapes=[
                pltpu.VMEM((len(parts) // len(SPLITS), src, orbs, aux, dom), jnp.bfloat16),
                pltpu.SemaphoreType.DMA((len(parts),)),
            ],
        ),
        out_shape=[shape] * len(begins),
        compiler_params=pltpu.CompilerParams(vmem_limit_bytes=VMEM),
        cost_estimate=pl.CostEstimate(
            flops=2 * count * len(begins) * src * aux * dom * dom * len(parts) // len(SPLITS),
            bytes_accessed=2 * src * orbs * aux * dom * len(parts) // len(SPLITS)
            + count * dom * dom * 4 * (len(begins) + sum(added)),
            transcendentals=0,
        ),
    )(pairs, jnp.stack(begins), *parts, *[b for b in bases if b is not None])


def fock_kernel(pairs_ref, begin_ref, slot_ref, occ_ref, len_ref, *refs):
    focks, amp_ref, base_ref, inv_ref, fock, sems = refs[:4], refs[4], *refs[5:]
    p = pl.program_id(0)
    dom = fock.shape[-1]

    @pl.when(p == 0)
    def _():
        each = focks[0].shape[0]
        copies = [
            pltpu.make_async_copy(
                focks[s], fock.at[s * each : (s + 1) * each], sems.at[s]
            )
            for s in range(4)
        ]
        for c in copies:
            c.start()
        for c in copies:
            c.wait()

    per = amp_ref.shape[0]
    for q in range(per):
        row = begin_ref[0] + p * per + q
        i = pairs_ref[2 * row]
        j = pairs_ref[2 * row + 1]
        energies = occ_ref[i] + occ_ref[j]
        old = amp_ref[q]
        fock_i = fock[slot_ref[i]]
        fock_j = fock[slot_ref[j]]
        total = jnp.dot(fock_i, old, preferred_element_type=jnp.float32)
        total += lax.dot_general(
            old, fock_j, (((1,), (1,)), ((), ())), preferred_element_type=jnp.float32
        )
        base_ref[q] = total - energies * old.astype(jnp.float32)
        rows = lax.broadcasted_iota(jnp.int32, (dom, dom), 0)
        columns = lax.broadcasted_iota(jnp.int32, (dom, dom), 1)
        eye = rows == columns
        diag_i = jnp.sum(
            jnp.where(eye, fock_i.astype(jnp.float32), 0.0), axis=1, keepdims=True
        )
        diag_j = jnp.sum(
            jnp.where(eye, fock_j.astype(jnp.float32), 0.0), axis=0, keepdims=True
        )
        inside = (rows < len_ref[i]) & (columns < len_ref[j])
        inv_ref[q] = jnp.where(inside, 1.0 / (diag_i + diag_j - energies), 0.0)


def fock_terms(focks, amplitudes, pairs, begin, slot, occ, lengths):
    count, dom, _ = amplitudes.shape
    one = pl.BlockSpec((PER, dom, dom), lambda p, *_: (p, 0, 0))
    shape = jax.ShapeDtypeStruct((count, dom, dom), jnp.float32)
    return pl.pallas_call(
        fock_kernel,
        grid_spec=pltpu.PrefetchScalarGridSpec(
            num_scalar_prefetch=5,
            grid=(count // PER,),
            in_specs=[pl.BlockSpec(memory_space=pl.ANY)] * 4 + [one],
            out_specs=[one, one],
            scratch_shapes=[
                pltpu.VMEM((4 * focks[0].shape[0], dom, dom), jnp.bfloat16),
                pltpu.SemaphoreType.DMA((4,)),
            ],
        ),
        out_shape=[shape, shape],
        compiler_params=pltpu.CompilerParams(vmem_limit_bytes=VMEM),
        cost_estimate=pl.CostEstimate(
            flops=2 * count * 2 * dom * dom * dom,
            bytes_accessed=count * dom * dom * 12,
            transcendentals=0,
        ),
    )(pairs, begin, slot, occ, lengths, *focks, amplitudes)


def finish_kernel(own_ref, other_ref, amp_ref, inv_ref, *refs):
    resid_ref, new_ref = refs[-2:]
    per = own_ref.shape[0]
    p = pl.program_id(0)
    for q in range(per):
        inv = inv_ref[q]
        inside = inv != 0.0
        resid = jnp.where(inside, own_ref[q] + decode(other_ref, p * per + q), 0.0)
        old = amp_ref[q].astype(jnp.float32)
        resid_ref[q] = resid.astype(resid_ref.dtype)
        new_ref[q] = jnp.where(inside, old - resid * inv, 0.0).astype(new_ref.dtype)


def finish(own, other, amplitudes, inv, first, held):
    total, dom, _ = amplitudes.shape
    count = (other.shape[0] - TAIL) // dom
    per = min(math.gcd(first, count), 2)
    shifted = pl.BlockSpec((per, dom, dom), lambda p: (p + first // per, 0, 0))
    shape = jax.ShapeDtypeStruct((total, dom, dom), jnp.bfloat16)
    extra = [] if held is None else list(held)
    return pl.pallas_call(
        finish_kernel,
        grid=(count // per,),
        in_specs=[
            shifted,
            pl.BlockSpec(other.shape, lambda p: (0, 0)),
            shifted,
            shifted,
        ]
        + [pl.BlockSpec(memory_space=pl.ANY)] * len(extra),
        out_specs=[shifted, shifted],
        out_shape=[shape, shape],
        input_output_aliases={4: 0, 5: 1} if extra else {},
        compiler_params=pltpu.CompilerParams(vmem_limit_bytes=VMEM),
        cost_estimate=pl.CostEstimate(
            flops=count * dom * dom * 5,
            bytes_accessed=count * dom * dom * 18,
            transcendentals=0,
        ),
    )(own, other, amplitudes, inv, *extra)


CHUNKS = ((0, 4), (4, 8), (8, 12), (12, 16))


def local(orbs, ys, integrals, fock_blocks, occ_energy, dom_len, amplitudes, pair_list):
    aux, occ, dom = integrals.shape
    group = occ // orbs
    owned = amplitudes.shape[0]
    y = lax.axis_index("pair")
    even = lax.rem(lax.axis_index("orb"), 2) == 0
    mate = jnp.where(even, 3 - y, y ^ 1)
    pairs = pair_list.reshape(-1)
    mine = (y * owned).astype(jnp.int32)
    theirs = (mate * owned).astype(jnp.int32)
    each = fock_blocks.shape[0]
    number = jnp.arange(group, dtype=jnp.int32)
    slot = ((number // each - y) & 3) * each + number % each
    focks = [fock_blocks] + [
        lax.ppermute(fock_blocks, "pair", [((s + shift) % ys, s) for s in range(ys)])
        for shift in (1, 2, 3)
    ]

    blocks = [arrange(integrals, orbs, lo, hi) for lo, hi in SPLITS]
    near, far = [], []
    for c in range(len(SPLITS)):
        block = blocks[c]
        if c == len(SPLITS) - 1:
            block, *focks = lax.optimization_barrier([block] + focks)
            base, inv = fock_terms(
                focks, amplitudes, pairs, mine.reshape(1), slot, occ_energy, dom_len
            )
        got = lax.all_to_all(block, "orb", split_axis=0, concat_axis=0, tiled=True)
        if c == 0:
            got, blocks[1] = lax.optimization_barrier((got, blocks[1]))
        if c == len(SPLITS) - 1:
            got, base, inv = lax.optimization_barrier((got, base, inv))
        near.append(got)
        far.append(exchange_with(got, gather_mate, orbs, ys))

    theirs_near, own = pair_sums(near, [None, base], pairs, [theirs, mine], [0, 0], owned)
    others = []
    for lo, hi in CHUNKS:
        sums = send_sums(far, theirs_near, pairs, theirs, lo, hi - lo)
        others.append(exchange_with(sums, sum_mate, orbs, ys))
    (own,) = pair_sums(far, [own], pairs, [mine], [0], owned)
    held = None
    for (lo, _), other in zip(CHUNKS, others):
        held = finish(own, other, amplitudes, inv, lo, held)
    return tuple(held)


def solution(mesh):
    placed = (
        P(("orb", "pair"), None, None),
        P(("orb", "pair"), None, None),
        P("orb"),
        P("orb"),
        P(("orb", "pair"), None, None),
        P("orb", None),
    )
    return jax.shard_map(
        functools.partial(local, mesh.shape["orb"], mesh.shape["pair"]),
        mesh=mesh,
        in_specs=placed,
        out_specs=(P(("orb", "pair"), None, None), P(("orb", "pair"), None, None)),
        check_vma=False,
    )
```

```python
import functools
import math

import jax
import jax.numpy as jnp
from jax import lax
from jax.experimental import pallas as pl
from jax.experimental.pallas import tpu as pltpu
from jax.sharding import PartitionSpec as P

BOTH = ("orb", "pair")
SPLITS = ((0, 12), (12, 16))
VMEM = 24 * 2**20
WIDE = 58 * 2**20
PIECES = 4
PER = 4
STEPS = 32767.0
TAIL = 16


def gather_mate(orb, y):
    return y ^ 1 if orb % 2 == 0 else 3 - y


def sum_mate(orb, y):
    return 3 - y if orb % 2 == 0 else y ^ 1


def exchange_with(x, mate, orbs, ys):
    pairs = [(o * ys + y, o * ys + mate(o, y)) for o in range(orbs) for y in range(ys)]
    return lax.ppermute(x, BOTH, pairs)


def arrange_kernel(lo, hi, x_ref, out_ref, x, out, sems, out_sems):
    aux, occ, dom = x.shape
    group = SPLITS[-1][1]
    each = occ // group // PIECES
    loads = [
        pltpu.make_async_copy(
            x_ref.at[:, k * each * group : (k + 1) * each * group],
            x.at[:, k * each * group : (k + 1) * each * group],
            sems.at[k],
        )
        for k in range(PIECES)
    ]
    for c in loads:
        c.start()
    size = ((hi - lo) * aux, aux * group)
    new = lax.broadcasted_iota(jnp.int32, size, 0)
    old = lax.broadcasted_iota(jnp.int32, size, 1)
    move = jnp.where((new % aux) * group + new // aux + lo == old, 1.0, 0.0).astype(x.dtype)
    stores = []
    for k in range(PIECES):
        loads[k].wait()
        for g in range(k * each, (k + 1) * each):
            block = x[:, g * group : (g + 1) * group, :].reshape(aux * group, dom)
            moved = jnp.dot(move, block, preferred_element_type=jnp.float32)
            out[g] = moved.astype(x.dtype).reshape(hi - lo, aux, dom)
        store = pltpu.make_async_copy(
            out.at[k * each : (k + 1) * each],
            out_ref.at[k * each : (k + 1) * each],
            out_sems.at[k],
        )
        store.start()
        stores.append(store)
    for c in stores:
        c.wait()


def arrange(integrals, orbs, lo, hi):
    aux, occ, dom = integrals.shape
    shape = (orbs, hi - lo, aux, dom)
    return pl.pallas_call(
        functools.partial(arrange_kernel, lo, hi),
        in_specs=[pl.BlockSpec(memory_space=pl.ANY)],
        out_specs=pl.BlockSpec(memory_space=pl.ANY),
        out_shape=jax.ShapeDtypeStruct(shape, integrals.dtype),
        scratch_shapes=[
            pltpu.VMEM(integrals.shape, integrals.dtype),
            pltpu.VMEM(shape, integrals.dtype),
            pltpu.SemaphoreType.DMA((PIECES,)),
            pltpu.SemaphoreType.DMA((PIECES,)),
        ],
        compiler_params=pltpu.CompilerParams(vmem_limit_bytes=WIDE),
        cost_estimate=pl.CostEstimate(
            flops=2 * orbs * (hi - lo) * aux * aux * (occ // orbs) * dom,
            bytes_accessed=2 * aux * occ * dom,
            transcendentals=0,
        ),
    )(integrals)


def load_blocks(parts, held, sems):
    return [
        pltpu.make_async_copy(part, held.at[c // len(SPLITS), :, lo:hi], sems.at[c])
        for c, (part, (lo, hi)) in enumerate(zip(parts, SPLITS * held.shape[0]))
    ]


def block_sum(held, i, j):
    total = None
    for h in range(held.shape[0]):
        left = held[h, :, i].reshape(-1, held.shape[-1])
        right = held[h, :, j].reshape(-1, held.shape[-1])
        term = lax.dot_general(
            left, right, (((0,), (0,)), ((), ())), preferred_element_type=jnp.float32
        )
        total = term if total is None else total + term
    return total


def column_tops(mantissa, power):
    return mantissa.astype(jnp.float32) * jnp.exp2(power.astype(jnp.float32))


def encode(totals, out_ref):
    dom = out_ref.shape[1]
    rows = lax.broadcasted_iota(jnp.int32, (TAIL, dom), 0)
    sizes = jnp.zeros((TAIL, dom), jnp.int32)
    for q, total in enumerate(totals):
        top = jnp.maximum(jnp.max(jnp.abs(total), axis=0, keepdims=True), 1e-30)
        power = jnp.floor(jnp.log2(top)).astype(jnp.int32) - 13
        mantissa = (top * jnp.exp2(-power.astype(jnp.float32))).astype(jnp.int32) + 1
        steps = jnp.round(total * (STEPS / column_tops(mantissa, power)))
        out_ref[q * dom : (q + 1) * dom, :] = steps.astype(jnp.int32).astype(jnp.int16)
        sizes = jnp.where(rows == 2 * q, mantissa, sizes)
        sizes = jnp.where(rows == 2 * q + 1, power, sizes)
    out_ref[len(totals) * dom :, :] = sizes.astype(jnp.int16)


def decode(code_ref, q):
    dom = code_ref.shape[1]
    rows = lax.broadcasted_iota(jnp.int32, (TAIL, dom), 0)
    sizes = code_ref[code_ref.shape[0] - TAIL :, :].astype(jnp.int32)
    mantissa = jnp.sum(jnp.where(rows == 2 * q, sizes, 0), axis=0, keepdims=True)
    power = jnp.sum(jnp.where(rows == 2 * q + 1, sizes, 0), axis=0, keepdims=True)
    start = pl.multiple_of(q * dom, dom)
    steps = code_ref[pl.ds(start, dom), :].astype(jnp.int32).astype(jnp.float32)
    return steps * (column_tops(mantissa, power) * (1.0 / STEPS))


def send_kernel(first, pairs_ref, begin_ref, *refs):
    parts, base_ref, out_ref, held, base, sems, base_sem = refs[:2], *refs[2:]
    count = base.shape[0]
    cut = SPLITS[0][1]
    bases = [
        pltpu.make_async_copy(base_ref.at[first + q], base.at[q], base_sem.at[q])
        for q in range(count)
    ]
    for q in range(count):
        row = begin_ref[0] + first + q
        for side in range(2):
            k = pairs_ref[2 * row + side]

            @pl.when(k < cut)
            def _():
                pltpu.make_async_copy(
                    parts[0].at[:, k], held.at[q, side], sems.at[q, side]
                ).start()

            @pl.when(k >= cut)
            def _():
                pltpu.make_async_copy(
                    parts[1].at[:, k - cut], held.at[q, side], sems.at[q, side]
                ).start()

        bases[q].start()
    totals = []
    for q in range(count):
        for side in range(2):
            pltpu.make_async_copy(
                parts[0].at[:, 0], held.at[q, side], sems.at[q, side]
            ).wait()
        bases[q].wait()
        left = held[q, 0].reshape(-1, held.shape[-1])
        right = held[q, 1].reshape(-1, held.shape[-1])
        term = lax.dot_general(
            left, right, (((0,), (0,)), ((), ())), preferred_element_type=jnp.float32
        )
        totals.append(base[q] + term)
    encode(totals, out_ref)


def send_sums(parts, base, pairs, begin, first, count):
    src, _, aux, dom = parts[0].shape
    return pl.pallas_call(
        functools.partial(send_kernel, first),
        in_specs=[pl.BlockSpec(memory_space=pltpu.SMEM)] * 2
        + [pl.BlockSpec(memory_space=pl.ANY)] * 3,
        out_specs=pl.BlockSpec(memory_space=pltpu.VMEM),
        out_shape=jax.ShapeDtypeStruct((count * dom + TAIL, dom), jnp.int16),
        scratch_shapes=[
            pltpu.VMEM((count, 2, src, aux, dom), jnp.bfloat16),
            pltpu.VMEM((count, dom, dom), jnp.float32),
            pltpu.SemaphoreType.DMA((count, 2)),
            pltpu.SemaphoreType.DMA((count,)),
        ],
        compiler_params=pltpu.CompilerParams(vmem_limit_bytes=VMEM),
        cost_estimate=pl.CostEstimate(
            flops=2 * count * src * aux * dom * dom,
            bytes_accessed=count * (4 * src * aux * dom + dom * dom * 6),
            transcendentals=0,
        ),
    )(pairs, begin.reshape(1), *parts, base)


def sums_kernel(rows, added, pairs_ref, begin_ref, *refs):
    held, sems = refs[-2:]
    count = held.shape[0] * len(SPLITS)
    parts, base_refs = refs[:count], refs[count : count + sum(added)]
    out_refs = refs[count + sum(added) : -2]
    p = pl.program_id(0)

    @pl.when(p == 0)
    def _():
        copies = load_blocks(parts, held, sems)
        for c in copies:
            c.start()
        for c in copies:
            c.wait()

    per = out_refs[0].shape[0]
    for q in range(per):
        bases = iter(base_refs)
        for k, (first, has) in enumerate(zip(rows, added)):
            row = begin_ref[k] + first + p * per + q
            total = block_sum(held, pairs_ref[2 * row], pairs_ref[2 * row + 1])
            if has:
                total += next(bases)[q]
            out_refs[k][q] = total


def pair_sums(parts, bases, pairs, begins, firsts, count, per=PER):
    src, _, aux, dom = parts[0].shape
    orbs = SPLITS[-1][1]
    added = tuple(b is not None for b in bases)
    in_specs = [pl.BlockSpec(memory_space=pl.ANY)] * len(parts) + [
        pl.BlockSpec((per, dom, dom), lambda p, *_, first=first: (p + first // per, 0, 0))
        for first, has in zip(firsts, added)
        if has
    ]
    shape = jax.ShapeDtypeStruct((count, dom, dom), jnp.float32)
    return pl.pallas_call(
        functools.partial(sums_kernel, tuple(firsts), added),
        grid_spec=pltpu.PrefetchScalarGridSpec(
            num_scalar_prefetch=2,
            grid=(count // per,),
            in_specs=in_specs,
            out_specs=[pl.BlockSpec((per,) + shape.shape[1:], lambda p, *_: (p, 0, 0))]
            * len(begins),
            scratch_shapes=[
                pltpu.VMEM((len(parts) // len(SPLITS), src, orbs, aux, dom), jnp.bfloat16),
                pltpu.SemaphoreType.DMA((len(parts),)),
            ],
        ),
        out_shape=[shape] * len(begins),
        compiler_params=pltpu.CompilerParams(vmem_limit_bytes=VMEM),
        cost_estimate=pl.CostEstimate(
            flops=2 * count * len(begins) * src * aux * dom * dom * len(parts) // len(SPLITS),
            bytes_accessed=2 * src * orbs * aux * dom * len(parts) // len(SPLITS)
            + count * dom * dom * 4 * (len(begins) + sum(added)),
            transcendentals=0,
        ),
    )(pairs, jnp.stack(begins), *parts, *[b for b in bases if b is not None])


def fock_kernel(pairs_ref, begin_ref, slot_ref, occ_ref, len_ref, *refs):
    focks, amp_ref, base_ref, inv_ref, fock, sems = refs[:4], refs[4], *refs[5:]
    p = pl.program_id(0)
    dom = fock.shape[-1]

    @pl.when(p == 0)
    def _():
        each = focks[0].shape[0]
        copies = [
            pltpu.make_async_copy(
                focks[s], fock.at[s * each : (s + 1) * each], sems.at[s]
            )
            for s in range(4)
        ]
        for c in copies:
            c.start()
        for c in copies:
            c.wait()

    per = amp_ref.shape[0]
    for q in range(per):
        row = begin_ref[0] + p * per + q
        i = pairs_ref[2 * row]
        j = pairs_ref[2 * row + 1]
        energies = occ_ref[i] + occ_ref[j]
        old = amp_ref[q]
        fock_i = fock[slot_ref[i]]
        fock_j = fock[slot_ref[j]]
        total = jnp.dot(fock_i, old, preferred_element_type=jnp.float32)
        total += lax.dot_general(
            old, fock_j, (((1,), (1,)), ((), ())), preferred_element_type=jnp.float32
        )
        base_ref[q] = total - energies * old.astype(jnp.float32)
        rows = lax.broadcasted_iota(jnp.int32, (dom, dom), 0)
        columns = lax.broadcasted_iota(jnp.int32, (dom, dom), 1)
        eye = rows == columns
        diag_i = jnp.sum(
            jnp.where(eye, fock_i.astype(jnp.float32), 0.0), axis=1, keepdims=True
        )
        diag_j = jnp.sum(
            jnp.where(eye, fock_j.astype(jnp.float32), 0.0), axis=0, keepdims=True
        )
        inside = (rows < len_ref[i]) & (columns < len_ref[j])
        inv_ref[q] = jnp.where(inside, 1.0 / (diag_i + diag_j - energies), 0.0)


def fock_terms(focks, amplitudes, pairs, begin, slot, occ, lengths):
    count, dom, _ = amplitudes.shape
    one = pl.BlockSpec((PER, dom, dom), lambda p, *_: (p, 0, 0))
    shape = jax.ShapeDtypeStruct((count, dom, dom), jnp.float32)
    return pl.pallas_call(
        fock_kernel,
        grid_spec=pltpu.PrefetchScalarGridSpec(
            num_scalar_prefetch=5,
            grid=(count // PER,),
            in_specs=[pl.BlockSpec(memory_space=pl.ANY)] * 4 + [one],
            out_specs=[one, one],
            scratch_shapes=[
                pltpu.VMEM((4 * focks[0].shape[0], dom, dom), jnp.bfloat16),
                pltpu.SemaphoreType.DMA((4,)),
            ],
        ),
        out_shape=[shape, shape],
        compiler_params=pltpu.CompilerParams(vmem_limit_bytes=VMEM),
        cost_estimate=pl.CostEstimate(
            flops=2 * count * 2 * dom * dom * dom,
            bytes_accessed=count * dom * dom * 12,
            transcendentals=0,
        ),
    )(pairs, begin, slot, occ, lengths, *focks, amplitudes)


def finish_kernel(own_ref, other_ref, amp_ref, inv_ref, *refs):
    resid_ref, new_ref = refs[-2:]
    per = own_ref.shape[0]
    p = pl.program_id(0)
    for q in range(per):
        inv = inv_ref[q]
        inside = inv != 0.0
        resid = jnp.where(inside, own_ref[q] + decode(other_ref, p * per + q), 0.0)
        old = amp_ref[q].astype(jnp.float32)
        resid_ref[q] = resid.astype(resid_ref.dtype)
        new_ref[q] = jnp.where(inside, old - resid * inv, 0.0).astype(new_ref.dtype)


def finish(own, other, amplitudes, inv, first, held):
    total, dom, _ = amplitudes.shape
    count = (other.shape[0] - TAIL) // dom
    per = min(math.gcd(first, count), 2)
    shifted = pl.BlockSpec((per, dom, dom), lambda p: (p + first // per, 0, 0))
    shape = jax.ShapeDtypeStruct((total, dom, dom), jnp.bfloat16)
    extra = [] if held is None else list(held)
    return pl.pallas_call(
        finish_kernel,
        grid=(count // per,),
        in_specs=[
            shifted,
            pl.BlockSpec(other.shape, lambda p: (0, 0)),
            shifted,
            shifted,
        ]
        + [pl.BlockSpec(memory_space=pl.ANY)] * len(extra),
        out_specs=[shifted, shifted],
        out_shape=[shape, shape],
        input_output_aliases={4: 0, 5: 1} if extra else {},
        compiler_params=pltpu.CompilerParams(vmem_limit_bytes=VMEM),
        cost_estimate=pl.CostEstimate(
            flops=count * dom * dom * 5,
            bytes_accessed=count * dom * dom * 18,
            transcendentals=0,
        ),
    )(own, other, amplitudes, inv, *extra)


CHUNKS = ((0, 4), (4, 8), (8, 12), (12, 16))


def local(orbs, ys, integrals, fock_blocks, occ_energy, dom_len, amplitudes, pair_list):
    aux, occ, dom = integrals.shape
    group = occ // orbs
    owned = amplitudes.shape[0]
    y = lax.axis_index("pair")
    even = lax.rem(lax.axis_index("orb"), 2) == 0
    mate = jnp.where(even, 3 - y, y ^ 1)
    pairs = pair_list.reshape(-1)
    mine = (y * owned).astype(jnp.int32)
    theirs = (mate * owned).astype(jnp.int32)
    each = fock_blocks.shape[0]
    number = jnp.arange(group, dtype=jnp.int32)
    slot = ((number // each - y) & 3) * each + number % each
    focks = [fock_blocks] + [
        lax.ppermute(fock_blocks, "pair", [((s + shift) % ys, s) for s in range(ys)])
        for shift in (1, 2, 3)
    ]

    blocks = [arrange(integrals, orbs, lo, hi) for lo, hi in SPLITS]
    near, far = [], []
    for c in range(len(SPLITS)):
        block = blocks[c]
        if c == len(SPLITS) - 1:
            block, *focks = lax.optimization_barrier([block] + focks)
            base, inv = fock_terms(
                focks, amplitudes, pairs, mine.reshape(1), slot, occ_energy, dom_len
            )
        got = lax.all_to_all(block, "orb", split_axis=0, concat_axis=0, tiled=True)
        if c == 0:
            got, blocks[1] = lax.optimization_barrier((got, blocks[1]))
        if c == len(SPLITS) - 1:
            got, base, inv = lax.optimization_barrier((got, base, inv))
        near.append(got)
        far.append(exchange_with(got, gather_mate, orbs, ys))

    theirs_near, own = pair_sums(near, [None, base], pairs, [theirs, mine], [0, 0], owned)
    others = []
    for lo, hi in CHUNKS:
        sums = send_sums(far, theirs_near, pairs, theirs, lo, hi - lo)
        others.append(exchange_with(sums, sum_mate, orbs, ys))
    (own,) = pair_sums(far, [own], pairs, [mine], [0], owned)
    held = None
    for (lo, _), other in zip(CHUNKS, others):
        held = finish(own, other, amplitudes, inv, lo, held)
    return tuple(held)


def solution(mesh):
    placed = (
        P(("orb", "pair"), None, None),
        P(("orb", "pair"), None, None),
        P("orb"),
        P("orb"),
        P(("orb", "pair"), None, None),
        P("orb", None),
    )
    return jax.shard_map(
        functools.partial(local, mesh.shape["orb"], mesh.shape["pair"]),
        mesh=mesh,
        in_specs=placed,
        out_specs=(P(("orb", "pair"), None, None), P(("orb", "pair"), None, None)),
        check_vma=False,
    )
```
